128 devices in a mesh: resp: 16 (over z, x_lo, core), exp: 8 (over y, x_hi).
Axes of the slice: x: 4 (x_hi: 2, x_lo: 2; x = x_hi * 2 + x_lo), y: 4, z: 4, core: 2. Of those that a mesh axis runs over, the one named last changes fastest.
Arguments:
- queries: bfloat16 [256, 32, 36864], P('resp', None, 'exp'), may hold values from -4 to 4
- resp_latent: bfloat16 [256, 32, 576], P('resp'), may hold values from -4 to 4
- prompt_cache: bfloat16 [16, 128, 576], P('resp'), may hold values from -4 to 4
- prompt_len: int32 [16], replicated, may hold values from 32 to 128, as said below
- w_uv: bfloat16 [64, 512, 128], P('exp'), may hold values from -0.25 to 0.25
- w_o: bfloat16 [8192, 7168], P('exp', 'resp'), may hold values from -0.0625 to 0.0625
- residual: bfloat16 [8192, 7168], P(('resp', 'exp')), may hold values from -3 to 3
- norm_gain: float32 [7168], replicated, may hold values from 0.1 to 1.9
- expert_in: bfloat16 [16, 2, 7168, 1024], P('resp', None, None, 'exp'), may hold values from -0.0625 to 0.0625
- expert_out: bfloat16 [16, 1024, 7168], P('resp', None, 'exp'), may hold values from -0.1875 to 0.1875
- routes: int32 [8192, 1], P(('resp', 'exp')), may hold values from 0 to 15; in each aligned block of 64 rows (0 to 63, 64 to 127, ...) at most 4 rows name the same one
- gate_probs: float32 [8192, 1], P(('resp', 'exp')), may hold values from 0.1 to 1
Outputs:
- layer_out: bfloat16 [8192, 7168], P(('resp', 'exp'))
The draws below stay inside these ranges and needn't reach their ends.
Inputs may be any that keep to these rules, and one draw needn't show every extreme that they name: `prompt_len`: some prompt has exactly 128 live entries. `routes`: among the rows of one device (aligned blocks of 64 rows) no expert is chosen more than 4 times, a bound that some block reaches.
All inputs are finite; a program needn't handle non-finite values.
Results may differ from the reference program's by a relative error of at most 0.029.
Values may be sent and summed in bfloat16 or wider, within the bound.
No kernel may reach another device: no remote copies, remote signals or barrier semaphores. Data moves between devices by JAX's collectives and lax.ppermute only.
A program may use at most 128 MiB of HBM per device.

```python
import math
import jax
import jax.numpy as jnp
import numpy as np
from jax import lax

D = 7168
H = 64
LAT = 512
ROPE = 64
VHEAD = 128
FF = 1024
TOP = 1
RLEN = 32
PLEN = 128
PROMPTS = 16
RESPONSES = 256
TOKENS = 8192
EXPERTS = 16
TOK_MOE = 64
CAP = 4
N_EXP = 8


def draw_queries(key, part):
    key = jax.random.fold_in(key, 11)
    shape = (RESPONSES, RLEN, H, LAT + ROPE)
    values = jnp.clip(jax.random.normal(key, shape, jnp.float32), -4.0, 4.0)
    return values.reshape(RESPONSES, RLEN, H * (LAT + ROPE)).astype(jnp.bfloat16)


def draw_prompt_cache(key, part):
    key = jax.random.fold_in(key, 23)
    shape = (PROMPTS, PLEN, LAT + ROPE)
    values = jnp.clip(jax.random.normal(key, shape, jnp.float32), -4.0, 4.0)
    return values.astype(jnp.bfloat16)


def draw_prompt_len(key, part):
    key = jax.random.fold_in(key, 37)
    length_key, longest_key = jax.random.split(key)
    lengths = jax.random.randint(length_key, (PROMPTS,), PLEN // 4, PLEN + 1)
    longest = jax.random.randint(longest_key, (), 0, PROMPTS)
    return jnp.where(jnp.arange(PROMPTS) == longest, PLEN, lengths).astype(jnp.int32)


def block_levels(key, shape, cuts, low, largest):
    def one(dim, blocks):
        heights = jax.random.uniform(jax.random.fold_in(jax.random.fold_in(key, 6), dim), (blocks,), jnp.float32, low / len(cuts), largest / len(cuts))
        return jnp.repeat(jnp.exp(heights), shape[dim] // blocks).reshape((-1,) + (1,) * (len(shape) - dim - 1))

    level = one(*cuts[0])
    for cut in cuts[1:]:
        level = level * one(*cut)
    return level


def assign_block(stream_key, own, number, rows, count, top, reach, slope):
    order = jax.random.permutation(stream_key, count)
    crowded, usual = portions_of(count, rows * top, reach, slope, True), portions_of(count, rows * top, reach, slope, False)
    places = jnp.arange(count)

    def named(sizes, turn):
        used = int((sizes > 0).sum())
        fixed = max(1, used // 4)
        passed = fixed + (places - fixed + turn * (used - fixed)) % max(1, count - fixed)
        return jnp.zeros((count,), jnp.int32).at[order[jnp.where(places < fixed, places, passed)]].set(jnp.asarray(sizes, jnp.int32))

    sizes = jnp.where(number % 4 == 0, named(crowded, number // 4), named(usual, number - number // 4 - 1))
    mixed = jax.random.permutation(jax.random.fold_in(own, 3), count)
    source_of, sink = mixed[0:count // 2 * 2:2], mixed[1:count // 2 * 2:2]
    margin = jnp.minimum(sizes[source_of] - 1, reach - sizes[sink]) // 2
    margin = jnp.where((source_of == order[0]) | (sink == order[0]) | (sizes[sink] == 0), 0, jnp.maximum(margin, 0))
    passed = jax.random.randint(jax.random.fold_in(own, 4), (count // 2,), 0, 1 << 20) % (margin + 1)
    sizes = sizes.at[source_of].add(-passed).at[sink].add(passed)
    items = jnp.searchsorted(jnp.cumsum(sizes), jnp.arange(rows * top), side="right").astype(jnp.int32)
    grid = items.reshape(top, rows).T
    grid = grid[jax.random.permutation(jax.random.fold_in(own, 1), rows)]
    turn = jax.random.randint(jax.random.fold_in(own, 2), (rows, 1), 0, top)
    return jnp.take_along_axis(grid, (jnp.arange(top)[None, :] + turn) % top, axis=1)


def portions_of(number_of, total, reach, lean, full):
    weights = [(1 << 20) // math.isqrt(grade ** lean) + 1 for grade in range(1, number_of + 1)]
    largest = reach if full else min(reach, max(-(-total // number_of), total * weights[0] // sum(weights)))
    least = 1 if total - largest >= number_of - 1 else 0
    counts, surplus = [largest] + [least] * (number_of - 1), total - largest - least * (number_of - 1)
    while surplus > 0:
        free = [i for i in range(1, number_of) if counts[i] < largest] or [i for i in range(1, number_of) if counts[i] < reach]
        whole, remaining = sum([weights[i] for i in free]), surplus
        for i in free:
            extra = min(reach - counts[i], max(1, remaining * weights[i] // whole), surplus)
            counts[i] = counts[i] + extra
            surplus = surplus - extra
    return np.array(counts)


def scatter_about(own_key, dims, deviation, most, pieces=(), kind=jnp.bfloat16):
    drawn = jax.random.normal(own_key, dims, jnp.float32) * deviation
    if len(pieces) > 0:
        drawn = block_levels(own_key, dims, pieces, -0.22, 0.18) * drawn
    return jnp.clip(drawn, min=-most, max=most).astype(kind)


def setup_inputs(seed: int = 0) -> dict:
    keys = jax.random.split(jax.random.key(seed), 13)
    queries = draw_queries(jax.random.fold_in(keys[12], 71), 0)
    resp_latent = scatter_about(keys[1], (RESPONSES, RLEN, LAT + ROPE), 1.0, 4.0, ((0, 16),))
    prompt_cache = draw_prompt_cache(jax.random.fold_in(keys[12], 71), 0)
    prompt_len = draw_prompt_len(jax.random.fold_in(keys[12], 71), 0)
    w_uv = scatter_about(keys[4], (H, LAT, VHEAD), LAT ** -0.5, 0.25, ((0, 8),))
    w_o = scatter_about(keys[5], (H * VHEAD, D), (H * VHEAD) ** -0.5, 0.0625, ((0, 8), (1, 16)))
    residual = scatter_about(keys[6], (TOKENS, D), 0.5, 3.0, ((0, 128),))
    norm_gain = jnp.clip(1.0 + 0.18 * jax.random.normal(keys[7], (D,), jnp.float32), 0.1, 1.9)
    expert_in = scatter_about(keys[8], (EXPERTS, 2, D, FF), D ** -0.5, 0.0625, ((0, 16), (3, 8)))
    expert_out = scatter_about(keys[9], (EXPERTS, FF, D), FF ** -0.5, 0.1875, ((0, 16), (2, 8)))
    routes_keys = jax.random.split(jax.random.fold_in(keys[10], 1), TOKENS // TOK_MOE)
    routes_turns = jax.random.permutation(jax.random.fold_in(keys[10], 3), TOKENS // TOK_MOE)
    routes = jax.vmap(lambda own, number: assign_block(jax.random.fold_in(keys[10], 2), own, number, TOK_MOE, EXPERTS, TOP, CAP, 2))(routes_keys, routes_turns).reshape((TOKENS, TOP))
    gate_probs = jnp.clip(jnp.exp(math.log(1.0) - 2.3025851 * jax.random.uniform(keys[11], (TOKENS, TOP), jnp.float32) ** block_levels(keys[11], (TOKENS, TOP), ((0, 128),), -0.2, 0.2)), 0.1, 1.0)
    return dict(queries=queries, resp_latent=resp_latent, prompt_cache=prompt_cache, prompt_len=prompt_len, w_uv=w_uv, w_o=w_o, residual=residual, norm_gain=norm_gain, expert_in=expert_in, expert_out=expert_out, routes=routes, gate_probs=gate_probs)


SCALE = 192.0 ** (-0.5)
ROUTED = 2.5
EPSILON = 1e-06
NEGATIVE = -1e+30

def reference(queries, resp_latent, prompt_cache, prompt_len, w_uv, w_o, residual, norm_gain, expert_in, expert_out, routes, gate_probs):
    entry_width = LAT + ROPE
    prompt_count = prompt_cache.shape[0]

    def one_response(response):
        prompt = (response % prompt_count).astype(jnp.int32)
        query_rows = queries[response].astype(jnp.float32).reshape(RLEN, H, entry_width)
        cache_rows = lax.dynamic_index_in_dim(prompt_cache, prompt, 0, keepdims=False).astype(jnp.float32)
        own_rows = resp_latent[response].astype(jnp.float32)
        key_rows = jnp.concatenate([cache_rows, own_rows], axis=0)
        live = lax.dynamic_index_in_dim(prompt_len, prompt, 0, keepdims=False)
        position = jnp.arange(PLEN + RLEN, dtype=jnp.int32)[None, :]
        query_pos = jnp.arange(RLEN, dtype=jnp.int32)[:, None]
        allowed = jnp.where(position < PLEN, position < live, position - PLEN <= query_pos)
        scores = jnp.einsum('thc,kc->htk', query_rows, key_rows, precision=lax.Precision.HIGHEST) * SCALE
        scores = jnp.where(allowed[None], scores, NEGATIVE)
        peak_score = lax.optimization_barrier(jnp.max(scores, axis=-1, keepdims=True))
        weights = jnp.exp(scores - peak_score)
        probabilities = weights / lax.optimization_barrier(jnp.sum(weights, axis=-1, keepdims=True))
        rounded = lax.optimization_barrier(probabilities.astype(jnp.bfloat16)).astype(jnp.float32)
        latent = jnp.einsum('htk,kc->thc', rounded, key_rows[:, :LAT], precision=lax.Precision.HIGHEST).astype(jnp.bfloat16)
        values = jnp.einsum('thc,hcv->thv', latent.astype(jnp.float32), w_uv.astype(jnp.float32), precision=lax.Precision.HIGHEST)
        return values.astype(jnp.bfloat16).reshape(RLEN, H * VHEAD)
    head_out = lax.map(one_response, jnp.arange(queries.shape[0], dtype=jnp.int32))
    head_out = head_out.reshape(-1, H * VHEAD)
    width = H // N_EXP * VHEAD
    attention = jnp.zeros((head_out.shape[0], D), jnp.float32)
    for group in range(N_EXP):
        share = jnp.dot(head_out[:, group * width:(group + 1) * width], w_o[group * width:(group + 1) * width], preferred_element_type=jnp.float32).astype(jnp.bfloat16)
        attention = attention + lax.optimization_barrier(share).astype(jnp.float32)
    hidden = residual.astype(jnp.float32) + attention
    scale_rows = lax.rsqrt(lax.optimization_barrier(jnp.mean(hidden * hidden, axis=-1, keepdims=True)) + EPSILON)
    normed = (hidden * scale_rows * norm_gain).astype(jnp.bfloat16)
    gate_share = ROUTED * gate_probs
    most_rows = CAP * (TOKENS // TOK_MOE)
    slot_range = jnp.arange(most_rows, dtype=jnp.int32)

    def one_expert(carried, expert):
        chosen = routes == expert
        weight = lax.optimization_barrier(jnp.sum(jnp.where(chosen, gate_share, 0.0), axis=-1))
        taken = jnp.any(chosen, axis=-1)
        live_rows = jnp.sum(taken.astype(jnp.int32))
        picked = jnp.nonzero(taken, size=most_rows, fill_value=0)[0].astype(jnp.int32)
        token_rows = normed[picked]
        gate_act = jnp.dot(token_rows, expert_in[expert, 0], preferred_element_type=jnp.float32)
        up_act = jnp.dot(token_rows, expert_in[expert, 1], preferred_element_type=jnp.float32)
        product = (jax.nn.silu(gate_act) * up_act).astype(jnp.bfloat16)
        result = jnp.dot(product, expert_out[expert], preferred_element_type=jnp.float32).astype(jnp.bfloat16)
        factor = jnp.where(slot_range < live_rows, weight[picked], 0.0)
        carried = carried.at[picked].add(factor[:, None] * result.astype(jnp.float32))
        return (carried, None)
    mixture, _ = lax.scan(one_expert, jnp.zeros(hidden.shape, jnp.float32), jnp.arange(EXPERTS, dtype=jnp.int32))
    return (hidden + mixture).astype(jnp.bfloat16)
```

```python
import functools

import jax
import jax.numpy as jnp
from jax import lax
from jax.experimental import pallas as pl
from jax.experimental.pallas import tpu as pltpu
from jax.sharding import PartitionSpec as P

SCALE = 192.0 ** (-0.5)
ROUTED = 2.5
EPSILON = 1e-06
NEGATIVE = -1e30
NZ, NX, NC, NY, NH = 4, 2, 2, 4, 2
RLEN, ENTRY, LAT, PLEN, HEADS, VHEAD = 32, 576, 512, 128, 8, 128
DIM, SLICE, HALF, FF, HID = 7168, 896, 448, 1024, 128
GROUP, BLOCK, EXPERTS, CAP = 512, 64, 16, 4
MESSAGE = 2 * FF + 128
BF = jnp.bfloat16
F32 = jnp.float32
VMEM_BYTES = 56 * 1024 * 1024


def params():
    return pltpu.CompilerParams(vmem_limit_bytes=VMEM_BYTES)


def resp_perm(dz, dx, dc):
    pairs = []
    for z in range(NZ):
        for x in range(NX):
            for c in range(NC):
                source = (z * NX + x) * NC + c
                target = (((z + dz) % NZ) * NX + (x ^ dx)) * NC + (c ^ dc)
                pairs.append((source, target))
    return pairs


def exp_perm(dy, dh):
    pairs = []
    for y in range(NY):
        for h in range(NH):
            pairs.append((y * NH + h, ((y + dy) % NY) * NH + (h ^ dh)))
    return pairs


def over_resp(x, dz, dx, dc):
    return lax.ppermute(x, "resp", resp_perm(dz, dx, dc))


def over_exp(x, dy, dh):
    return lax.ppermute(x, "exp", exp_perm(dy, dh))


def everywhere(z, x, c, y, h):
    return ((z * NX + x) * NC + c) * (NY * NH) + y * NH + h


def crossing():
    return [
        (everywhere(z, x, c, y, h), everywhere(-y % NZ, x, c, z, h))
        for z in range(NZ)
        for x in range(NX)
        for c in range(NC)
        for y in range(NY)
        for h in range(NH)
    ]


def diagonal():
    return [
        (everywhere(z, x, c, y, h), everywhere(z, x, 1 - c, y, 1 - h))
        for z in range(NZ)
        for x in range(NX)
        for c in range(NC)
        for y in range(NY)
        for h in range(NH)
    ]


def over_z(x, step):
    return over_resp(x, step, 0, 0)


def over_y(x, step):
    return over_exp(x, step, 0)


def ring(x, shift):
    half = x.shape[0] // 2
    left = shift(x, 1)
    right = shift(x, 3)
    return [x, left, shift(left[:half], 1), shift(right[half:], 3), right]


def dot(a, b):
    return lax.dot_general(a, b, (((1,), (0,)), ((), ())), preferred_element_type=F32)


def dot_nt(a, b):
    return lax.dot_general(a, b, (((1,), (1,)), ((), ())), preferred_element_type=F32)


def attention_kernel(lens, q_ref, keys, own, w_uv, out, lat, even, odd, bias):
    step = pl.program_id(0)
    rows = HEADS * RLEN
    total = PLEN + RLEN

    @pl.when(step == 0)
    def _():
        even[:, :, ENTRY:] = jnp.zeros((2, total, 640 - ENTRY), BF)
        odd[:, :, :64] = jnp.zeros((2, total, 64), BF)
        column = lax.broadcasted_iota(jnp.int32, (rows, total), 1)
        token = lax.broadcasted_iota(jnp.int32, (rows, total), 0) % RLEN
        seen = (column < PLEN) | (column <= token + PLEN)
        bias[...] = jnp.where(seen, 0.0, NEGATIVE)

    for part in range(2):
        resp = 2 * step + part
        even[part, :PLEN, :ENTRY] = keys[part]
        even[part, PLEN:, :ENTRY] = own[part]
        odd[part, :PLEN, 64:] = keys[part]
        odd[part, PLEN:, 64:] = own[part]
        first = [q_ref[part, :, p * 1152 : p * 1152 + 640] for p in range(HEADS // 2)]
        second = [q_ref[part, :, p * 1152 + 512 : p * 1152 + 1152] for p in range(HEADS // 2)]
        scores = jnp.concatenate(
            [
                dot_nt(jnp.concatenate(first, axis=0), even[part]),
                dot_nt(jnp.concatenate(second, axis=0), odd[part]),
            ],
            axis=0,
        )
        column = lax.broadcasted_iota(jnp.int32, (1, total), 1)
        dead = (column >= lens[resp]) & (column < PLEN)
        scores = scores + (bias[...] + jnp.where(dead, NEGATIVE, 0.0))
        peak = jnp.max(scores, axis=1, keepdims=True)
        weights = jnp.exp((scores - peak) * SCALE)
        probs = (weights * (1.0 / jnp.sum(weights, axis=1, keepdims=True))).astype(BF)
        latent = dot(probs, even[part, :, :LAT]).astype(BF)
        start = pl.multiple_of(resp * RLEN, RLEN)
        for p in range(HEADS // 2):
            lat[2 * p, pl.ds(start, RLEN), :] = latent[p * RLEN : (p + 1) * RLEN]
            lat[2 * p + 1, pl.ds(start, RLEN), :] = latent[
                rows // 2 + p * RLEN : rows // 2 + (p + 1) * RLEN
            ]

    @pl.when(step == pl.num_programs(0) - 1)
    def _():
        for head in range(HEADS):
            out[:, head * VHEAD : (head + 1) * VHEAD] = dot(lat[head], w_uv[head]).astype(BF)


def attention(lens, queries, keys, own, w_uv):
    count = queries.shape[0]
    spec = pltpu.PrefetchScalarGridSpec(
        num_scalar_prefetch=1,
        grid=(count // 2,),
        in_specs=[
            pl.BlockSpec((2, RLEN, HEADS * ENTRY), lambda i, n: (i, 0, 0)),
            pl.BlockSpec((2, PLEN, ENTRY), lambda i, n: (i, 0, 0)),
            pl.BlockSpec((2, RLEN, ENTRY), lambda i, n: (i, 0, 0)),
            pl.BlockSpec((HEADS, LAT, VHEAD), lambda i, n: (0, 0, 0)),
        ],
        out_specs=pl.BlockSpec((GROUP, HEADS * VHEAD), lambda i, n: (0, 0)),
        scratch_shapes=[
            pltpu.VMEM((HEADS, GROUP, LAT), BF),
            pltpu.VMEM((2, PLEN + RLEN, 640), BF),
            pltpu.VMEM((2, PLEN + RLEN, 640), BF),
            pltpu.VMEM((HEADS * RLEN, PLEN + RLEN), F32),
        ],
    )
    return pl.pallas_call(
        attention_kernel,
        grid_spec=spec,
        out_shape=jax.ShapeDtypeStruct((GROUP, HEADS * VHEAD), BF),
        compiler_params=params(),
        name="attention",
    )(lens, queries, keys, own, w_uv)


def project_kernel(side, first_match, *refs):
    heads, weights = refs[:10], refs[10:20]
    out, v_all, w_all, v_sem, w_sem = refs[20:]
    half = GROUP // 2
    cut = HALF // 2

    def head_copies(k):
        copies = []
        for core in range(2):
            own = heads[5 * core : 5 * core + 5]
            base = core * GROUP
            if k == 2:
                copies.append((own[2], v_all.at[k, pl.ds(base, half)], 4 * core + 2))
                copies.append((own[3], v_all.at[k, pl.ds(base + half, half)], 8 + core))
            else:
                source = own[k] if k < 2 else own[4]
                copies.append((source, v_all.at[k, pl.ds(base, GROUP)], 4 * core + k))
        return [pltpu.make_async_copy(a, b, v_sem.at[n]) for a, b, n in copies]

    def weight_copies(k, which):
        own = weights[5 * which : 5 * which + 5]
        copies = []
        if k == 2:
            copies.append((own[2], w_all.at[k, pl.ds(0, cut)], 2))
            copies.append((own[3], w_all.at[k, pl.ds(cut, cut)], 4))
        else:
            source = own[k] if k < 2 else own[4]
            copies.append((source, w_all.at[k], k))
        return [pltpu.make_async_copy(a, b, w_sem.at[n]) for a, b, n in copies]

    for k in range(NZ):
        for which in range(2):

            @pl.when(side[0] == which)
            def _(k=k, which=which):
                for copy in weight_copies(k, which):
                    copy.start()

        for copy in head_copies(k):
            copy.start()
    for k in range(NZ):
        for copy in weight_copies(k, 0):
            copy.wait()
        for copy in head_copies(k):
            copy.wait()
    tile = 256
    for t in range(2 * GROUP // tile):
        total = None
        for k in range(NZ):
            match = (first_match[0] + 2 * NZ - k) % NY
            term = dot_nt(w_all[k], v_all[match, t * tile : (t + 1) * tile, :])
            total = term if total is None else total + term
        out[:, t * tile : (t + 1) * tile] = total.astype(BF)


def project(side, first_match, heads, weights):
    vmem = pl.BlockSpec(memory_space=pltpu.VMEM)
    smem = pl.BlockSpec(memory_space=pltpu.SMEM)
    anywhere = pl.BlockSpec(memory_space=pl.ANY)
    return pl.pallas_call(
        project_kernel,
        in_specs=[smem, smem] + [anywhere] * 20,
        out_specs=vmem,
        out_shape=jax.ShapeDtypeStruct((HALF, 2 * GROUP), BF),
        scratch_shapes=[
            pltpu.VMEM((NY, 2 * GROUP, HEADS * VHEAD), BF),
            pltpu.VMEM((NZ, HALF, HEADS * VHEAD), BF),
            pltpu.SemaphoreType.DMA((10,)),
            pltpu.SemaphoreType.DMA((5,)),
        ],
        compiler_params=params(),
        name="project",
    )(side, first_match, *heads, *weights)


def dispatch_kernel(core, kept, sent, kept_far, sent_far, rest, place, out, attended):
    near = kept[:, :GROUP].astype(F32) + sent[...].astype(F32)
    far = kept_far[...].astype(F32) + sent_far[...].astype(F32)
    lower = core[0] == 0
    attended[:HALF, :] = jnp.where(lower, near, far).astype(BF)
    attended[HALF:, :] = jnp.where(lower, far, near).astype(BF)
    rows = lax.broadcasted_iota(jnp.int32, (GROUP, GROUP), 0)
    select = jnp.where(rows == place[...], 1.0, 0.0).astype(BF)
    moved = dot(select, rest[...])
    out[:, :SLICE] = (moved[:, :SLICE] + dot_nt(select, attended[...])).astype(BF)
    out[:, SLICE:] = moved[:, SLICE:].astype(BF)


def dispatch(core, kept, sent, kept_far, sent_far, rest, place):
    vmem = pl.BlockSpec(memory_space=pltpu.VMEM)
    return pl.pallas_call(
        dispatch_kernel,
        in_specs=[pl.BlockSpec(memory_space=pltpu.SMEM)] + [vmem] * 6,
        out_specs=vmem,
        out_shape=jax.ShapeDtypeStruct((GROUP, SLICE + 128), BF),
        scratch_shapes=[pltpu.VMEM((SLICE, GROUP), BF)],
        compiler_params=params(),
        name="dispatch",
    )(core, kept, sent, kept_far, sent_far, rest, place)


def enter_kernel(tokens, gain, weights, out):
    hidden = tokens[:, :SLICE].astype(F32)
    square = jnp.sum(hidden * hidden, axis=1, keepdims=True)
    scaled = (hidden * gain[...]).astype(BF)
    for k in range(FF // HID):
        out[:, k * 2 * HID : (k + 1) * 2 * HID] = dot(
            scaled, weights[k * SLICE : (k + 1) * SLICE, :]
        ).astype(BF)
    high = square.astype(BF)
    low = (square - high.astype(F32)).astype(BF)
    lane = lax.broadcasted_iota(jnp.int32, (GROUP, 128), 1)
    out[:, 2 * FF :] = jnp.where(lane < 64, high.astype(F32), low.astype(F32)).astype(BF)


def enter(tokens, gain, weights):
    vmem = pl.BlockSpec(memory_space=pltpu.VMEM)
    return pl.pallas_call(
        enter_kernel,
        in_specs=[vmem] * 3,
        out_specs=vmem,
        out_shape=jax.ShapeDtypeStruct((GROUP, MESSAGE), BF),
        compiler_params=params(),
        name="enter",
    )(tokens, gain, weights)


def act_kernel(parts, out):
    total = parts[:BLOCK, :].astype(F32)
    for k in range(1, GROUP // BLOCK):
        total = total + parts[k * BLOCK : (k + 1) * BLOCK, :].astype(F32)
    square = total[:, 2 * FF : 2 * FF + 1] + total[:, 2 * FF + 64 : 2 * FF + 65]
    scale = lax.rsqrt(square * (1.0 / DIM) + EPSILON)
    for k in range(FF // HID):
        gate = total[:, 2 * k * HID : (2 * k + 1) * HID] * scale
        up = total[:, (2 * k + 1) * HID : (2 * k + 2) * HID] * scale
        act = (gate / (1.0 + jnp.exp(-gate)) * up).astype(BF)
        for b in range(GROUP // BLOCK):
            out[b * BLOCK : (b + 1) * BLOCK, k * HID : (k + 1) * HID] = act


def activate(parts):
    vmem = pl.BlockSpec(memory_space=pltpu.VMEM)
    return pl.pallas_call(
        act_kernel,
        in_specs=[vmem],
        out_specs=vmem,
        out_shape=jax.ShapeDtypeStruct((GROUP, FF), BF),
        compiler_params=params(),
        name="activate",
    )(parts)


def leave_kernel(act, w_out, tokens, out):
    result = dot(act[...], w_out[0]).astype(BF).astype(F32)
    parts = tokens[:, SLICE:].astype(F32)
    share = ROUTED * (parts[:, 1:2] + parts[:, 2:3] + parts[:, 3:4])
    out[...] = (tokens[:, :SLICE].astype(F32) + share * result).astype(BF)


def leave(act, w_out, tokens):
    vmem = pl.BlockSpec(memory_space=pltpu.VMEM)
    return pl.pallas_call(
        leave_kernel,
        in_specs=[vmem] * 3,
        out_specs=vmem,
        out_shape=jax.ShapeDtypeStruct((GROUP, SLICE), BF),
        compiler_params=params(),
        name="leave",
    )(act, w_out, tokens)


def restore_kernel(rows, place, out):
    lane = lax.broadcasted_iota(jnp.int32, (BLOCK, GROUP), 1)
    data = rows[...]
    for k in range(DIM // SLICE):
        select = jnp.where(lane == place[...] + k * CAP, 1.0, 0.0).astype(BF)
        out[:, k * SLICE : (k + 1) * SLICE] = dot(select, data).astype(BF)


def restore(rows, place):
    vmem = pl.BlockSpec(memory_space=pltpu.VMEM)
    return pl.pallas_call(
        restore_kernel,
        in_specs=[vmem] * 2,
        out_specs=vmem,
        out_shape=jax.ShapeDtypeStruct((BLOCK, DIM), BF),
        compiler_params=params(),
        name="restore",
    )(rows, place)


def body(
    queries,
    resp_latent,
    prompt_cache,
    prompt_len,
    w_uv,
    w_o,
    residual,
    norm_gain,
    expert_in,
    expert_out,
    routes,
    gate_probs,
):
    r = lax.axis_index("resp")
    e = lax.axis_index("exp")
    z, x, c = r // 4, (r // 2) % 2, r % 2
    y, h = e // 2, e % 2

    keys = lax.all_gather(prompt_cache, "resp", axis=0, tiled=True)

    near_w = ring(lax.ppermute(w_o.T, ("resp", "exp"), crossing()), over_z)
    side_w = ring(over_resp(near_w[0], 0, 1, 0), over_z)

    both = jnp.concatenate([expert_in[0, 0], expert_in[0, 1]], axis=1)
    enter_w = lax.all_to_all(both, "exp", split_axis=0, concat_axis=0, tiled=True)

    first = gate_probs.astype(BF)
    second = (gate_probs - first.astype(F32)).astype(BF)
    third = (gate_probs - first.astype(F32) - second.astype(F32)).astype(BF)
    extra = jnp.concatenate([routes.astype(BF), first, second, third], axis=1)
    extra = jnp.pad(extra, ((0, 0), (0, 124)))
    extra = jnp.broadcast_to(extra[None], (8, BLOCK, 128))
    rest = residual.reshape(BLOCK, 8, SLICE).transpose(1, 0, 2)
    rest = jnp.concatenate([rest, extra], axis=2).reshape(GROUP, SLICE + 128)
    rest = lax.all_to_all(rest, "exp", split_axis=0, concat_axis=0, tiled=True)

    table = rest[:, SLICE].astype(jnp.int32).reshape(8, BLOCK)
    earlier = jnp.arange(BLOCK)[None, :] < jnp.arange(BLOCK)[:, None]
    same = (table[:, :, None] == table[:, None, :]) & earlier[None]
    rank = jnp.sum(same.astype(jnp.int32), axis=2)
    place = table * (8 * CAP) + jnp.arange(8, dtype=jnp.int32)[:, None] * CAP + rank
    place = place.reshape(1, GROUP)
    own_same = (routes == routes[:, 0][None, :]) & earlier
    own_place = routes * (8 * CAP) + jnp.sum(own_same.astype(jnp.int32), axis=1, keepdims=True)
    gain = lax.dynamic_slice_in_dim(norm_gain, e * SLICE, SLICE, 0).reshape(1, SLICE)

    values = attention(prompt_len, queries, keys, resp_latent, w_uv)
    heads = ring(values, over_y)
    heads = heads + [over_resp(piece, 0, 0, 1) for piece in heads]

    first_match = ((y + z) % NY).reshape(1).astype(jnp.int32)
    away = jnp.where(h == x, 1, 0).reshape(1).astype(jnp.int32)
    sent = project(away, first_match, heads, near_w + side_w)
    kept = project(1 - away, first_match, heads, near_w + side_w)
    sent_near = over_exp(sent[:, :GROUP], 0, 1)
    sent_far = lax.ppermute(sent[:, GROUP:], ("resp", "exp"), diagonal())
    kept_far = over_resp(kept[:, GROUP:], 0, 0, 1)
    core = c.reshape(1).astype(jnp.int32)
    sorted_rows = dispatch(core, kept, sent_near, kept_far, sent_far, rest, place)
    tokens = lax.all_to_all(sorted_rows, "resp", split_axis=0, concat_axis=0, tiled=True)
    message = enter(tokens, gain, enter_w)
    message = lax.all_to_all(message, "exp", split_axis=0, concat_axis=0, tiled=True)
    act = activate(message)
    act = lax.all_to_all(act, "exp", split_axis=0, concat_axis=0, tiled=True)
    finished = leave(act, expert_out, tokens)
    finished = lax.all_to_all(
        finished.reshape(128, CAP, SLICE),
        ("resp", "exp"),
        split_axis=0,
        concat_axis=0,
        tiled=True,
    ).reshape(GROUP, SLICE)
    return restore(finished, own_place)


def solution(mesh):
    return jax.shard_map(
        body,
        mesh=mesh,
        in_specs=(
            P("resp", None, "exp"),
            P("resp", None, None),
            P("resp", None, None),
            P(),
            P("exp", None, None),
            P("exp", "resp"),
            P(("resp", "exp"), None),
            P(),
            P("resp", None, None, "exp"),
            P("resp", None, "exp"),
            P(("resp", "exp"), None),
            P(("resp", "exp"), None),
        ),
        out_specs=P(("resp", "exp"), None),
        check_vma=False,
    )
```

```python
import functools

import jax
import jax.numpy as jnp
from jax import lax
from jax.experimental import pallas as pl
from jax.experimental.pallas import tpu as pltpu
from jax.sharding import PartitionSpec as P

SCALE = 192.0 ** (-0.5)
ROUTED = 2.5
EPSILON = 1e-06
NEGATIVE = -1e30
NZ, NX, NC, NY, NH = 4, 2, 2, 4, 2
RLEN, ENTRY, LAT, PLEN, HEADS, VHEAD = 32, 576, 512, 128, 8, 128
DIM, SLICE, HALF, FF, HID = 7168, 896, 448, 1024, 128
GROUP, BLOCK, CAP = 512, 64, 4
TILES = 2 * FF // 128 + 1
WEIGHTS = SLICE + 4 * BLOCK
ALONG_Y = [[y * NH + h for y in range(NY)] for h in range(NH)]
BF = jnp.bfloat16
F32 = jnp.float32


def params(mebibytes):
    return pltpu.CompilerParams(vmem_limit_bytes=mebibytes * 1024 * 1024)


def resp_perm(dz, dx, dc):
    pairs = []
    for z in range(NZ):
        for x in range(NX):
            for c in range(NC):
                source = (z * NX + x) * NC + c
                target = (((z + dz) % NZ) * NX + (x ^ dx)) * NC + (c ^ dc)
                pairs.append((source, target))
    return pairs


def exp_perm(dy, dh):
    pairs = []
    for y in range(NY):
        for h in range(NH):
            pairs.append((y * NH + h, ((y + dy) % NY) * NH + (h ^ dh)))
    return pairs


def over_resp(x, dz, dx, dc):
    return lax.ppermute(x, "resp", resp_perm(dz, dx, dc))


def over_exp(x, dy, dh):
    return lax.ppermute(x, "exp", exp_perm(dy, dh))


def everywhere(move):
    def number(z, x, c, y, h):
        return ((z * NX + x) * NC + c) * (NY * NH) + y * NH + h

    return [
        (number(z, x, c, y, h), number(*move(z, x, c, y, h)))
        for z in range(NZ)
        for x in range(NX)
        for c in range(NC)
        for y in range(NY)
        for h in range(NH)
    ]


def over_all(x, move):
    return lax.ppermute(x, ("resp", "exp"), everywhere(move))


def other_core(x, step):
    return over_all(x, lambda z, x, c, y, h: (z, x, 1 - c, (y + step) % NY, h))


def over_z(x, step):
    return over_resp(x, step, 0, 0)


def over_y(x, step):
    return over_exp(x, step, 0)


def after(x, y):
    return lax.optimization_barrier((x, y))


def near_pieces(x, shift):
    return [shift(x, 1), shift(x, 3)]


def ring_pieces(x, near, shift):
    half = x.shape[0] // 2
    left, right = near
    return [x, left, shift(left[:half], 1), shift(right[half:], 3), right]


def dot(a, b):
    return lax.dot_general(a, b, (((1,), (0,)), ((), ())), preferred_element_type=F32)


def dot_nt(a, b):
    return lax.dot_general(a, b, (((1,), (1,)), ((), ())), preferred_element_type=F32)


def attention_kernel(lens, q_ref, keys, own, w_uv, out, lat, even, odd, bias):
    step = pl.program_id(0)
    rows = HEADS * RLEN
    total = PLEN + RLEN

    @pl.when(step == 0)
    def _():
        even[:, PLEN:, ENTRY:] = jnp.zeros((2, RLEN, 640 - ENTRY), BF)
        odd[:, :, :64] = jnp.zeros((2, total, 64), BF)
        column = lax.broadcasted_iota(jnp.int32, (rows, total), 1)
        token = lax.broadcasted_iota(jnp.int32, (rows, total), 0) % RLEN
        seen = (column < PLEN) | (column <= token + PLEN)
        bias[...] = jnp.where(seen, 0.0, NEGATIVE)

    for part in range(2):
        resp = 2 * step + part
        even[part, :PLEN, :] = keys[part]
        even[part, PLEN:, :ENTRY] = own[part]
        odd[part, :PLEN, 64:] = keys[part, :, :ENTRY]
        odd[part, PLEN:, 64:] = own[part]
        first = [q_ref[part, :, p * 1152 : p * 1152 + 640] for p in range(HEADS // 2)]
        second = [q_ref[part, :, p * 1152 + 512 : p * 1152 + 1152] for p in range(HEADS // 2)]
        scores = jnp.concatenate(
            [
                dot_nt(jnp.concatenate(first, axis=0), even[part]),
                dot_nt(jnp.concatenate(second, axis=0), odd[part]),
            ],
            axis=0,
        )
        column = lax.broadcasted_iota(jnp.int32, (1, total), 1)
        dead = (column >= lens[resp]) & (column < PLEN)
        scores = scores + (bias[...] + jnp.where(dead, NEGATIVE, 0.0))
        peak = jnp.max(scores, axis=1, keepdims=True)
        weights = jnp.exp((scores - peak) * SCALE)
        probs = (weights * (1.0 / jnp.sum(weights, axis=1, keepdims=True))).astype(BF)
        latent = dot(probs, even[part, :, :LAT]).astype(BF)
        start = pl.multiple_of(resp * RLEN, RLEN)
        for p in range(HEADS // 2):
            lat[2 * p, pl.ds(start, RLEN), :] = latent[p * RLEN : (p + 1) * RLEN]
            lat[2 * p + 1, pl.ds(start, RLEN), :] = latent[
                rows // 2 + p * RLEN : rows // 2 + (p + 1) * RLEN
            ]

    @pl.when(step == pl.num_programs(0) - 1)
    def _():
        for head in range(HEADS):
            out[:, head * VHEAD : (head + 1) * VHEAD] = dot(lat[head], w_uv[head]).astype(BF)


def attention(lens, queries, keys, own, w_uv):
    count = queries.shape[0]
    spec = pltpu.PrefetchScalarGridSpec(
        num_scalar_prefetch=1,
        grid=(count // 2,),
        in_specs=[
            pl.BlockSpec((2, RLEN, HEADS * ENTRY), lambda i, n: (i, 0, 0)),
            pl.BlockSpec((2, PLEN, 640), lambda i, n: (i, 0, 0)),
            pl.BlockSpec((2, RLEN, ENTRY), lambda i, n: (i, 0, 0)),
            pl.BlockSpec((HEADS, LAT, VHEAD), lambda i, n: (0, 0, 0)),
        ],
        out_specs=pl.BlockSpec((GROUP, HEADS * VHEAD), lambda i, n: (0, 0)),
        scratch_shapes=[
            pltpu.VMEM((HEADS, GROUP, LAT), BF),
            pltpu.VMEM((2, PLEN + RLEN, 640), BF),
            pltpu.VMEM((2, PLEN + RLEN, 640), BF),
            pltpu.VMEM((HEADS * RLEN, PLEN + RLEN), F32),
        ],
    )
    return pl.pallas_call(
        attention_kernel,
        grid_spec=spec,
        out_shape=jax.ShapeDtypeStruct((GROUP, HEADS * VHEAD), BF),
        compiler_params=params(56),
        name="attention",
    )(lens, queries, keys, own, w_uv)


def project_kernel(count, by_rows, match, picks, *refs):
    heads, weights = refs[:4], refs[4:14]
    outs = refs[14 : 14 + 2 * count]
    v_all, w_all, v_sem, w_sem = refs[14 + 2 * count :]
    cut = HALF // 2

    def weight_copies(n, part, k):
        own = weights[5 * part : 5 * part + 5]
        copies = []
        for side in range(2):
            if k == 2:
                source = own[2 + side]
            else:
                source = own[min(k, 1) if k < 2 else 4].at[pl.ds(side * cut, cut)]
            target = w_all.at[n, part, pl.ds(side * cut, cut)]
            copies.append(pltpu.make_async_copy(source, target, w_sem.at[n, part, side]))
        return copies

    def start_weights(n):
        for k in range(NZ):

            @pl.when(picks[n] == k)
            def _():
                for part in range(2):
                    for copy in weight_copies(n, part, k):
                        copy.start()

    def head_copy(k):
        target = v_all.at[k // 2, pl.ds((k % 2) * GROUP, GROUP)]
        return pltpu.make_async_copy(heads[k], target, v_sem.at[k])

    start_weights(0)
    for k in range(4):
        head_copy(k).start()
    for n in range(1, count):
        start_weights(n)
    for k in range(4):
        head_copy(k).wait()
    for n in range(count):
        for part in range(2):
            for copy in weight_copies(n, part, 0):
                copy.wait()
        for core in range(2):
            total = None
            for part in range(2):
                group = v_all.at[match[0] if part == 0 else 1 - match[0]]
                term = dot_nt(w_all[n, part], group[core * GROUP : (core + 1) * GROUP, :])
                total = term if total is None else total + term
            total = total.astype(BF)
            if by_rows:
                for side in range(2):
                    outs[side][:, core * GROUP : (core + 1) * GROUP] = total[
                        side * cut : (side + 1) * cut
                    ]
            else:
                outs[2 * n + core][...] = total


def project(match, picks, heads, weights, by_rows=False):
    count = picks.shape[0]
    shape = (HALF // 2, 2 * GROUP) if by_rows else (HALF, GROUP)
    vmem = pl.BlockSpec(memory_space=pltpu.VMEM)
    smem = pl.BlockSpec(memory_space=pltpu.SMEM)
    anywhere = pl.BlockSpec(memory_space=pl.ANY)
    return pl.pallas_call(
        functools.partial(project_kernel, count, by_rows),
        in_specs=[smem, smem] + [anywhere] * 14,
        out_specs=[vmem] * (2 * count),
        out_shape=[jax.ShapeDtypeStruct(shape, BF)] * (2 * count),
        scratch_shapes=[
            pltpu.VMEM((2, 2 * GROUP, HEADS * VHEAD), BF),
            pltpu.VMEM((count, 2, HALF, HEADS * VHEAD), BF),
            pltpu.SemaphoreType.DMA((4,)),
            pltpu.SemaphoreType.DMA((count, 2, 2)),
        ],
        compiler_params=params(56),
        name="project",
    )(match, picks, *heads, *weights)


def merge_kernel(ahead0, ahead1, behind0, behind1, left, right, *outs):
    cut = HALF // 2
    for core, (ahead, behind) in enumerate(((ahead0, behind0), (ahead1, behind1))):
        lanes = slice(core * GROUP, (core + 1) * GROUP)
        first = ahead[:cut, :].astype(F32) + left[:, lanes].astype(F32)
        last = behind[cut:, :].astype(F32) + right[:, lanes].astype(F32)
        outs[core][:cut, :] = first.astype(BF)
        outs[core][cut:, :] = ahead[cut:, :]
        outs[2 + core][:cut, :] = behind[:cut, :]
        outs[2 + core][cut:, :] = last.astype(BF)


def merge(pieces, left, right):
    vmem = pl.BlockSpec(memory_space=pltpu.VMEM)
    return pl.pallas_call(
        merge_kernel,
        in_specs=[vmem] * 6,
        out_specs=[vmem] * 4,
        out_shape=[jax.ShapeDtypeStruct((HALF, GROUP), BF)] * 4,
        compiler_params=params(56),
        name="merge",
    )(*pieces, left, right)


def dispatch_kernel(core, near0, near1, near3, far0, far1, far3, rest, place, out, attended):
    near = near0[...].astype(F32) + near1[...].astype(F32) + near3[...].astype(F32)
    far = far0[...].astype(F32) + far1[...].astype(F32) + far3[...].astype(F32)
    lower = core[0] == 0
    attended[:HALF, :] = jnp.where(lower, near, far).astype(BF)
    attended[HALF:, :] = jnp.where(lower, far, near).astype(BF)
    rows = lax.broadcasted_iota(jnp.int32, (GROUP, GROUP), 0)
    select = jnp.where(rows == place[...], 1.0, 0.0).astype(BF)
    moved = dot(select, rest[...])
    out[:, :SLICE] = (moved[:, :SLICE] + dot_nt(select, attended[...])).astype(BF)
    out[:, SLICE:] = moved[:, SLICE:].astype(BF)


def dispatch(core, parts, rest, place):
    vmem = pl.BlockSpec(memory_space=pltpu.VMEM)
    return pl.pallas_call(
        dispatch_kernel,
        in_specs=[pl.BlockSpec(memory_space=pltpu.SMEM)] + [vmem] * 8,
        out_specs=vmem,
        out_shape=jax.ShapeDtypeStruct((GROUP, SLICE + 128), BF),
        scratch_shapes=[pltpu.VMEM((SLICE, GROUP), BF)],
        compiler_params=params(56),
        name="dispatch",
    )(core, *parts, rest, place)


def enter_kernel(half, tokens, gain, kept, come, out):
    hidden = tokens[:, :SLICE].astype(F32)
    square = jnp.sum(hidden * hidden, axis=1, keepdims=True)
    scaled = (hidden * gain[...]).astype(BF)

    def store(tile, value):
        for b in range(GROUP // BLOCK):
            start = pl.multiple_of((b * TILES + tile) * BLOCK, BLOCK)
            out[pl.ds(start, BLOCK), :] = value[b * BLOCK : (b + 1) * BLOCK]

    for k in range(NY):
        for weights, own in ((kept, half[0]), (come, 1 - half[0])):
            both = dot(scaled, weights[k, :SLICE, :]).astype(BF)
            for side in range(2):
                store((k * NH + own) * 2 + side, both[:, side * HID : (side + 1) * HID])
    high = square.astype(BF)
    low = (square - high.astype(F32)).astype(BF)
    lane = lax.broadcasted_iota(jnp.int32, (GROUP, 128), 1)
    store(TILES - 1, jnp.where(lane < 64, high.astype(F32), low.astype(F32)).astype(BF))


def enter(half, tokens, gain, kept, come):
    vmem = pl.BlockSpec(memory_space=pltpu.VMEM)
    return pl.pallas_call(
        enter_kernel,
        in_specs=[pl.BlockSpec(memory_space=pltpu.SMEM)] + [vmem] * 4,
        out_specs=vmem,
        out_shape=jax.ShapeDtypeStruct((GROUP * TILES, 128), BF),
        compiler_params=params(20),
        name="enter",
    )(half, tokens, gain, kept, come)


def act_kernel(parts, out):
    def total(tile):
        value = jnp.zeros((BLOCK, 128), F32)
        for k in range(GROUP // BLOCK):
            start = (k * TILES + tile) * BLOCK
            value = value + parts[start : start + BLOCK, :].astype(F32)
        return value

    square = total(TILES - 1)
    square = square[:, :1] + square[:, 64:65]
    scale = lax.rsqrt(square * (1.0 / DIM) + EPSILON)
    for k in range(FF // HID):
        gate = total(2 * k) * scale
        act = (gate / (1.0 + jnp.exp(-gate)) * (total(2 * k + 1) * scale)).astype(BF)
        for b in range(GROUP // BLOCK):
            out[b * BLOCK : (b + 1) * BLOCK, k * HID : (k + 1) * HID] = act


def activate(parts):
    vmem = pl.BlockSpec(memory_space=pltpu.VMEM)
    return pl.pallas_call(
        act_kernel,
        in_specs=[vmem],
        out_specs=vmem,
        out_shape=jax.ShapeDtypeStruct((GROUP, FF), BF),
        compiler_params=params(16),
        name="activate",
    )(parts)


def leave_kernel(act, w_out, tokens, out):
    result = dot(act[...], w_out[0]).astype(BF).astype(F32)
    parts = tokens[:, SLICE:].astype(F32)
    share = ROUTED * (parts[:, 1:2] + parts[:, 2:3] + parts[:, 3:4])
    out[...] = (tokens[:, :SLICE].astype(F32) + share * result).astype(BF)


def leave(act, w_out, tokens):
    vmem = pl.BlockSpec(memory_space=pltpu.VMEM)
    return pl.pallas_call(
        leave_kernel,
        in_specs=[vmem] * 3,
        out_specs=vmem,
        out_shape=jax.ShapeDtypeStruct((GROUP, SLICE), BF),
        compiler_params=params(16),
        name="leave",
    )(act, w_out, tokens)


def restore_kernel(rows, place, out, select):
    lane = lax.broadcasted_iota(jnp.int32, (BLOCK, GROUP), 1)
    count = DIM // SLICE
    for k in range(count):
        select[k * BLOCK : (k + 1) * BLOCK, :] = jnp.where(
            lane == place[...] + k * CAP, 1.0, 0.0
        ).astype(BF)
    moved = dot(select[...], rows[...]).astype(BF)
    for k in range(count):
        out[:, k * SLICE : (k + 1) * SLICE] = moved[k * BLOCK : (k + 1) * BLOCK]


def restore(rows, place):
    vmem = pl.BlockSpec(memory_space=pltpu.VMEM)
    return pl.pallas_call(
        restore_kernel,
        in_specs=[vmem] * 2,
        out_specs=vmem,
        out_shape=jax.ShapeDtypeStruct((BLOCK, DIM), BF),
        scratch_shapes=[pltpu.VMEM((GROUP, GROUP), BF)],
        compiler_params=params(8),
        name="restore",
    )(rows, place)


def body(
    queries,
    resp_latent,
    prompt_cache,
    prompt_len,
    w_uv,
    w_o,
    residual,
    norm_gain,
    expert_in,
    expert_out,
    routes,
    gate_probs,
):
    r = lax.axis_index("resp")
    e = lax.axis_index("exp")
    z, x, c = r // 4, (r // 2) % 2, r % 2
    y, h = e // 2, e % 2

    cache = jnp.pad(prompt_cache, ((0, 0), (0, 0), (0, 640 - ENTRY)))
    keys = lax.all_gather(cache, "resp", axis=0, tiled=True)

    first_base = over_all(w_o.T, lambda z, x, c, y, h: (z, h, c, y, x))
    second_base = over_resp(first_base, 0, 1, 0)
    first_near = near_pieces(first_base, over_z)
    first_w = ring_pieces(first_base, first_near, over_z)
    second_near = near_pieces(second_base, over_z)
    second_w = ring_pieces(second_base, second_near, over_z)

    both = jnp.concatenate([expert_in[0, 0], expert_in[0, 1]], axis=1)

    first = gate_probs.astype(BF)
    second = (gate_probs - first.astype(F32)).astype(BF)
    third = (gate_probs - first.astype(F32) - second.astype(F32)).astype(BF)
    extra = jnp.concatenate([routes.astype(BF), first, second, third], axis=1)
    extra = jnp.pad(extra, ((0, 0), (0, 124)))
    extra = jnp.broadcast_to(extra[None], (8, BLOCK, 128))
    rest = residual.reshape(BLOCK, 8, SLICE).transpose(1, 0, 2)
    rest = jnp.concatenate([rest, extra], axis=2).reshape(8, 4 * BLOCK, 256)
    both = jnp.concatenate([both.reshape(8, SLICE, 256), rest], axis=1)
    both, _ = after(both, first_base)
    both = lax.all_to_all(
        both, "exp", split_axis=0, concat_axis=0, axis_index_groups=ALONG_Y, tiled=True
    ).reshape(NY, NH, WEIGHTS, 256)

    def half_of(which):
        return lax.dynamic_index_in_dim(both, which, 1, keepdims=False)


    values = attention(prompt_len, queries, keys, resp_latent, w_uv)
    values, _ = after(values, first_near + [second_base])
    others = over_exp(values, 0, 1)
    gone, _ = after(half_of(1 - h), [others] + second_near + first_w)
    come, kept = over_exp(gone, 0, 1), half_of(h)
    rest = [data[:, SLICE:] for data in (kept, come)]
    rest = jnp.stack(
        [jnp.where(h == 0, rest[0], rest[1]), jnp.where(h == 0, rest[1], rest[0])], axis=1
    ).reshape(GROUP, SLICE + 128)
    others, _ = after(others, second_near + first_w)
    heads = [values, over_resp(values, 0, 0, 1), others, over_resp(others, 0, 0, 1)]

    table = rest[:, SLICE].astype(jnp.int32).reshape(8, BLOCK)
    earlier = jnp.arange(BLOCK)[None, :] < jnp.arange(BLOCK)[:, None]
    same = (table[:, :, None] == table[:, None, :]) & earlier[None]
    rank = jnp.sum(same.astype(jnp.int32), axis=2)
    place = table * (8 * CAP) + jnp.arange(8, dtype=jnp.int32)[:, None] * CAP + rank
    place = place.reshape(1, GROUP)
    gain = lax.dynamic_slice_in_dim(norm_gain, e * SLICE, SLICE, 0).reshape(1, SLICE)
    own_same = (routes == routes[:, 0][None, :]) & earlier
    own_place = routes * (8 * CAP) + jnp.sum(own_same.astype(jnp.int32), axis=1, keepdims=True)

    match = jnp.where(h == x, 0, 1).reshape(1).astype(jnp.int32)
    pick = [((z - y - dy + 2 * NY) % NY).astype(jnp.int32) for dy in range(NY)]
    top, bottom = project(match, jnp.stack(pick[2:3]), heads, first_w + second_w, True)
    from_left = over_exp(top, 1, 0)
    from_right = over_exp(bottom, 3, 0)
    order = jnp.stack([pick[1], pick[3], pick[0]])
    pieces = project(match, order, heads, first_w + second_w)
    near1, far1, near3, far3 = merge(pieces[:4], from_left, from_right)
    parts = [
        pieces[4],
        over_exp(near1, 1, 0),
        over_exp(near3, 3, 0),
        other_core(pieces[5], 0),
        other_core(far1, 1),
        other_core(far3, 3),
    ]
    core = c.reshape(1).astype(jnp.int32)
    sorted_rows = dispatch(core, parts, rest, place)
    tokens = lax.all_to_all(sorted_rows, "resp", split_axis=0, concat_axis=0, tiled=True)
    message = enter(h.reshape(1).astype(jnp.int32), tokens, gain, kept, come)
    message = lax.all_to_all(message, "exp", split_axis=0, concat_axis=0, tiled=True)
    act = activate(message)
    act = lax.all_to_all(act, "exp", split_axis=0, concat_axis=0, tiled=True)
    finished = leave(act, expert_out, tokens)
    finished = lax.all_to_all(
        finished.reshape(128, CAP, SLICE),
        ("resp", "exp"),
        split_axis=0,
        concat_axis=0,
        tiled=True,
    ).reshape(GROUP, SLICE)
    return restore(finished, own_place)


def solution(mesh):
    return jax.shard_map(
        body,
        mesh=mesh,
        in_specs=(
            P("resp", None, "exp"),
            P("resp", None, None),
            P("resp", None, None),
            P(),
            P("exp", None, None),
            P("exp", "resp"),
            P(("resp", "exp"), None),
            P(),
            P("resp", None, None, "exp"),
            P("resp", None, "exp"),
            P(("resp", "exp"), None),
            P(("resp", "exp"), None),
        ),
        out_specs=P(("resp", "exp"), None),
        check_vma=False,
    )
```

```python
import functools

import jax
import jax.numpy as jnp
from jax import lax
from jax.experimental import pallas as pl
from jax.experimental.pallas import tpu as pltpu
from jax.sharding import PartitionSpec as P

SCALE = 192.0 ** (-0.5)
ROUTED = 2.5
EPSILON = 1e-06
NEGATIVE = -1e30
NZ, NX, NC, NY, NH = 4, 2, 2, 4, 2
RLEN, ENTRY, LAT, PLEN, HEADS, VHEAD = 32, 576, 512, 128, 8, 128
DIM, SLICE, HALF, FF, HID = 7168, 896, 448, 1024, 128
GROUP, BLOCK, CAP = 512, 64, 4
BATCH = 4
TILES = 2 * FF // 128 + 1
WEIGHTS = SLICE + 4 * BLOCK
ALONG_Y = [[y * NH + h for y in range(NY)] for h in range(NH)]
BF = jnp.bfloat16
F32 = jnp.float32


def params(mebibytes):
    return pltpu.CompilerParams(vmem_limit_bytes=mebibytes * 1024 * 1024)


def resp_perm(dz, dx, dc):
    pairs = []
    for z in range(NZ):
        for x in range(NX):
            for c in range(NC):
                source = (z * NX + x) * NC + c
                target = (((z + dz) % NZ) * NX + (x ^ dx)) * NC + (c ^ dc)
                pairs.append((source, target))
    return pairs


def exp_perm(dy, dh):
    pairs = []
    for y in range(NY):
        for h in range(NH):
            pairs.append((y * NH + h, ((y + dy) % NY) * NH + (h ^ dh)))
    return pairs


def over_resp(x, dz, dx, dc):
    return lax.ppermute(x, "resp", resp_perm(dz, dx, dc))


def over_exp(x, dy, dh):
    return lax.ppermute(x, "exp", exp_perm(dy, dh))


def everywhere(move):
    def number(z, x, c, y, h):
        return ((z * NX + x) * NC + c) * (NY * NH) + y * NH + h

    return [
        (number(z, x, c, y, h), number(*move(z, x, c, y, h)))
        for z in range(NZ)
        for x in range(NX)
        for c in range(NC)
        for y in range(NY)
        for h in range(NH)
    ]


def over_all(x, move):
    return lax.ppermute(x, ("resp", "exp"), everywhere(move))


def other_core(x, step):
    return over_all(x, lambda z, x, c, y, h: (z, x, 1 - c, (y + step) % NY, h))


def over_z(x, step):
    return over_resp(x, step, 0, 0)


def over_y(x, step):
    return over_exp(x, step, 0)


def after(x, y):
    return lax.optimization_barrier((x, y))


def near_pieces(x, shift):
    return [shift(x, 1), shift(x, 3)]


def ring_pieces(x, near, shift):
    half = x.shape[0] // 2
    left, right = near
    return [x, left, shift(left[:half], 1), shift(right[half:], 3), right]


def dot(a, b):
    return lax.dot_general(a, b, (((1,), (0,)), ((), ())), preferred_element_type=F32)


def dot_nt(a, b):
    return lax.dot_general(a, b, (((1,), (1,)), ((), ())), preferred_element_type=F32)


def attention_kernel(lens, q_ref, keys, own, w_uv, out, lat, even, odd, bias):
    step = pl.program_id(0)
    rows = HEADS * RLEN
    total = PLEN + RLEN

    @pl.when(step == 0)
    def _():
        even[:, PLEN:, ENTRY:] = jnp.zeros((BATCH, RLEN, 640 - ENTRY), BF)
        odd[:, :, :64] = jnp.zeros((BATCH, total, 64), BF)
        column = lax.broadcasted_iota(jnp.int32, (rows, total), 1)
        token = lax.broadcasted_iota(jnp.int32, (rows, total), 0) % RLEN
        seen = (column < PLEN) | (column <= token + PLEN)
        bias[...] = jnp.where(seen, 0.0, NEGATIVE)

    for part in range(BATCH):
        resp = BATCH * step + part
        even[part, :PLEN, :] = keys[part]
        even[part, PLEN:, :ENTRY] = own[part]
        odd[part, :PLEN, 64:] = keys[part, :, :ENTRY]
        odd[part, PLEN:, 64:] = own[part]
        first = [q_ref[part, :, p * 1152 : p * 1152 + 640] for p in range(HEADS // 2)]
        second = [q_ref[part, :, p * 1152 + 512 : p * 1152 + 1152] for p in range(HEADS // 2)]
        scores = jnp.concatenate(
            [
                dot_nt(jnp.concatenate(first, axis=0), even[part]),
                dot_nt(jnp.concatenate(second, axis=0), odd[part]),
            ],
            axis=0,
        )
        column = lax.broadcasted_iota(jnp.int32, (1, total), 1)
        dead = (column >= lens[resp]) & (column < PLEN)
        scores = scores + (bias[...] + jnp.where(dead, NEGATIVE, 0.0))
        peak = jnp.max(scores, axis=1, keepdims=True)
        weights = jnp.exp((scores - peak) * SCALE)
        probs = (weights * (1.0 / jnp.sum(weights, axis=1, keepdims=True))).astype(BF)
        latent = dot(probs, even[part, :, :LAT]).astype(BF)
        start = pl.multiple_of(resp * RLEN, RLEN)
        for p in range(HEADS // 2):
            lat[2 * p, pl.ds(start, RLEN), :] = latent[p * RLEN : (p + 1) * RLEN]
            lat[2 * p + 1, pl.ds(start, RLEN), :] = latent[
                rows // 2 + p * RLEN : rows // 2 + (p + 1) * RLEN
            ]

    @pl.when(step == pl.num_programs(0) - 1)
    def _():
        for head in range(HEADS):
            out[:, head * VHEAD : (head + 1) * VHEAD] = dot(lat[head], w_uv[head]).astype(BF)


def attention(lens, queries, keys, own, w_uv):
    count = queries.shape[0]
    spec = pltpu.PrefetchScalarGridSpec(
        num_scalar_prefetch=1,
        grid=(count // BATCH,),
        in_specs=[
            pl.BlockSpec((BATCH, RLEN, HEADS * ENTRY), lambda i, n: (i, 0, 0)),
            pl.BlockSpec((BATCH, PLEN, 640), lambda i, n: (i, 0, 0)),
            pl.BlockSpec((BATCH, RLEN, ENTRY), lambda i, n: (i, 0, 0)),
            pl.BlockSpec((HEADS, LAT, VHEAD), lambda i, n: (0, 0, 0)),
        ],
        out_specs=pl.BlockSpec((GROUP, HEADS * VHEAD), lambda i, n: (0, 0)),
        scratch_shapes=[
            pltpu.VMEM((HEADS, GROUP, LAT), BF),
            pltpu.VMEM((BATCH, PLEN + RLEN, 640), BF),
            pltpu.VMEM((BATCH, PLEN + RLEN, 640), BF),
            pltpu.VMEM((HEADS * RLEN, PLEN + RLEN), F32),
        ],
    )
    return pl.pallas_call(
        attention_kernel,
        grid_spec=spec,
        out_shape=jax.ShapeDtypeStruct((GROUP, HEADS * VHEAD), BF),
        compiler_params=params(56),
        name="attention",
    )(lens, queries, keys, own, w_uv)


def project_kernel(count, by_rows, match, picks, *refs):
    heads, weights = refs[:4], refs[4:14]
    outs = refs[14 : 14 + 2 * count]
    v_all, w_all, v_sem, w_sem = refs[14 + 2 * count :]
    cut = HALF // 2

    def weight_copies(n, part, k):
        own = weights[5 * part : 5 * part + 5]
        copies = []
        for side in range(2):
            if k == 2:
                source = own[2 + side]
            else:
                source = own[min(k, 1) if k < 2 else 4].at[pl.ds(side * cut, cut)]
            target = w_all.at[n, part, pl.ds(side * cut, cut)]
            copies.append(pltpu.make_async_copy(source, target, w_sem.at[n, part, side]))
        return copies

    def start_weights(n):
        for k in range(NZ):

            @pl.when(picks[n] == k)
            def _():
                for part in range(2):
                    for copy in weight_copies(n, part, k):
                        copy.start()

    def head_copy(k):
        target = v_all.at[k // 2, pl.ds((k % 2) * GROUP, GROUP)]
        return pltpu.make_async_copy(heads[k], target, v_sem.at[k])

    start_weights(0)
    for k in range(4):
        head_copy(k).start()
    for n in range(1, count):
        start_weights(n)
    for k in range(4):
        head_copy(k).wait()
    for n in range(count):
        for part in range(2):
            for copy in weight_copies(n, part, 0):
                copy.wait()
        for core in range(2):
            total = None
            for part in range(2):
                group = v_all.at[match[0] if part == 0 else 1 - match[0]]
                term = dot_nt(w_all[n, part], group[core * GROUP : (core + 1) * GROUP, :])
                total = term if total is None else total + term
            total = total.astype(BF)
            if by_rows:
                for side in range(2):
                    outs[side][:, core * GROUP : (core + 1) * GROUP] = total[
                        side * cut : (side + 1) * cut
                    ]
            else:
                outs[2 * n + core][...] = total


def project(match, picks, heads, weights, by_rows=False):
    count = picks.shape[0]
    shape = (HALF // 2, 2 * GROUP) if by_rows else (HALF, GROUP)
    vmem = pl.BlockSpec(memory_space=pltpu.VMEM)
    smem = pl.BlockSpec(memory_space=pltpu.SMEM)
    anywhere = pl.BlockSpec(memory_space=pl.ANY)
    return pl.pallas_call(
        functools.partial(project_kernel, count, by_rows),
        in_specs=[smem, smem] + [anywhere] * 14,
        out_specs=[vmem] * (2 * count),
        out_shape=[jax.ShapeDtypeStruct(shape, BF)] * (2 * count),
        scratch_shapes=[
            pltpu.VMEM((2, 2 * GROUP, HEADS * VHEAD), BF),
            pltpu.VMEM((count, 2, HALF, HEADS * VHEAD), BF),
            pltpu.SemaphoreType.DMA((4,)),
            pltpu.SemaphoreType.DMA((count, 2, 2)),
        ],
        compiler_params=params(56),
        name="project",
    )(match, picks, *heads, *weights)


def merge_kernel(ahead0, ahead1, behind0, behind1, left, right, *outs):
    cut = HALF // 2
    for core, (ahead, behind) in enumerate(((ahead0, behind0), (ahead1, behind1))):
        lanes = slice(core * GROUP, (core + 1) * GROUP)
        first = ahead[:cut, :].astype(F32) + left[:, lanes].astype(F32)
        last = behind[cut:, :].astype(F32) + right[:, lanes].astype(F32)
        outs[core][:cut, :] = first.astype(BF)
        outs[core][cut:, :] = ahead[cut:, :]
        outs[2 + core][:cut, :] = behind[:cut, :]
        outs[2 + core][cut:, :] = last.astype(BF)


def merge(pieces, left, right):
    vmem = pl.BlockSpec(memory_space=pltpu.VMEM)
    return pl.pallas_call(
        merge_kernel,
        in_specs=[vmem] * 6,
        out_specs=[vmem] * 4,
        out_shape=[jax.ShapeDtypeStruct((HALF, GROUP), BF)] * 4,
        compiler_params=params(56),
        name="merge",
    )(*pieces, left, right)


def dispatch_kernel(core, near0, near1, near3, far0, far1, far3, rest, place, out, attended):
    near = near0[...].astype(F32) + near1[...].astype(F32) + near3[...].astype(F32)
    far = far0[...].astype(F32) + far1[...].astype(F32) + far3[...].astype(F32)
    lower = core[0] == 0
    attended[:HALF, :] = jnp.where(lower, near, far).astype(BF)
    attended[HALF:, :] = jnp.where(lower, far, near).astype(BF)
    rows = lax.broadcasted_iota(jnp.int32, (GROUP, GROUP), 0)
    select = jnp.where(rows == place[...], 1.0, 0.0).astype(BF)
    moved = dot(select, rest[...])
    out[:, :SLICE] = (moved[:, :SLICE] + dot_nt(select, attended[...])).astype(BF)
    out[:, SLICE:] = moved[:, SLICE:].astype(BF)


def dispatch(core, parts, rest, place):
    vmem = pl.BlockSpec(memory_space=pltpu.VMEM)
    return pl.pallas_call(
        dispatch_kernel,
        in_specs=[pl.BlockSpec(memory_space=pltpu.SMEM)] + [vmem] * 8,
        out_specs=vmem,
        out_shape=jax.ShapeDtypeStruct((GROUP, SLICE + 128), BF),
        scratch_shapes=[pltpu.VMEM((SLICE, GROUP), BF)],
        compiler_params=params(56),
        name="dispatch",
    )(core, *parts, rest, place)


def enter_kernel(half, tokens, gain, kept, come, out):
    hidden = tokens[:, :SLICE].astype(F32)
    square = jnp.sum(hidden * hidden, axis=1, keepdims=True)
    scaled = (hidden * gain[...]).astype(BF)

    def store(tile, value):
        for b in range(GROUP // BLOCK):
            start = pl.multiple_of((b * TILES + tile) * BLOCK, BLOCK)
            out[pl.ds(start, BLOCK), :] = value[b * BLOCK : (b + 1) * BLOCK]

    for k in range(NY):
        for weights, own in ((kept, half[0]), (come, 1 - half[0])):
            both = dot(scaled, weights[k, :SLICE, :]).astype(BF)
            for side in range(2):
                store((k * NH + own) * 2 + side, both[:, side * HID : (side + 1) * HID])
    high = square.astype(BF)
    low = (square - high.astype(F32)).astype(BF)
    lane = lax.broadcasted_iota(jnp.int32, (GROUP, 128), 1)
    store(TILES - 1, jnp.where(lane < 64, high.astype(F32), low.astype(F32)).astype(BF))


def enter(half, tokens, gain, kept, come):
    vmem = pl.BlockSpec(memory_space=pltpu.VMEM)
    return pl.pallas_call(
        enter_kernel,
        in_specs=[pl.BlockSpec(memory_space=pltpu.SMEM)] + [vmem] * 4,
        out_specs=vmem,
        out_shape=jax.ShapeDtypeStruct((GROUP * TILES, 128), BF),
        compiler_params=params(20),
        name="enter",
    )(half, tokens, gain, kept, come)


def act_kernel(parts, out):
    def total(tile):
        value = jnp.zeros((BLOCK, 128), F32)
        for k in range(GROUP // BLOCK):
            start = (k * TILES + tile) * BLOCK
            value = value + parts[start : start + BLOCK, :].astype(F32)
        return value

    square = total(TILES - 1)
    square = square[:, :1] + square[:, 64:65]
    scale = lax.rsqrt(square * (1.0 / DIM) + EPSILON)
    for k in range(FF // HID):
        gate = total(2 * k) * scale
        act = (gate / (1.0 + jnp.exp(-gate)) * (total(2 * k + 1) * scale)).astype(BF)
        for b in range(GROUP // BLOCK):
            out[b * BLOCK : (b + 1) * BLOCK, k * HID : (k + 1) * HID] = act


def activate(parts):
    vmem = pl.BlockSpec(memory_space=pltpu.VMEM)
    return pl.pallas_call(
        act_kernel,
        in_specs=[vmem],
        out_specs=vmem,
        out_shape=jax.ShapeDtypeStruct((GROUP, FF), BF),
        compiler_params=params(16),
        name="activate",
    )(parts)


def leave_kernel(act, w_out, tokens, out):
    result = dot(act[...], w_out[0]).astype(BF).astype(F32)
    parts = tokens[:, SLICE:].astype(F32)
    share = ROUTED * (parts[:, 1:2] + parts[:, 2:3] + parts[:, 3:4])
    out[...] = (tokens[:, :SLICE].astype(F32) + share * result).astype(BF)


def leave(act, w_out, tokens):
    vmem = pl.BlockSpec(memory_space=pltpu.VMEM)
    return pl.pallas_call(
        leave_kernel,
        in_specs=[vmem] * 3,
        out_specs=vmem,
        out_shape=jax.ShapeDtypeStruct((GROUP, SLICE), BF),
        compiler_params=params(16),
        name="leave",
    )(act, w_out, tokens)


def restore_kernel(rows, place, out, select):
    lane = lax.broadcasted_iota(jnp.int32, (BLOCK, GROUP), 1)
    count = DIM // SLICE
    for k in range(count):
        select[k * BLOCK : (k + 1) * BLOCK, :] = jnp.where(
            lane == place[...] + k * CAP, 1.0, 0.0
        ).astype(BF)
    moved = dot(select[...], rows[...]).astype(BF)
    for k in range(count):
        out[:, k * SLICE : (k + 1) * SLICE] = moved[k * BLOCK : (k + 1) * BLOCK]


def restore(rows, place):
    vmem = pl.BlockSpec(memory_space=pltpu.VMEM)
    return pl.pallas_call(
        restore_kernel,
        in_specs=[vmem] * 2,
        out_specs=vmem,
        out_shape=jax.ShapeDtypeStruct((BLOCK, DIM), BF),
        scratch_shapes=[pltpu.VMEM((GROUP, GROUP), BF)],
        compiler_params=params(8),
        name="restore",
    )(rows, place)


def body(
    queries,
    resp_latent,
    prompt_cache,
    prompt_len,
    w_uv,
    w_o,
    residual,
    norm_gain,
    expert_in,
    expert_out,
    routes,
    gate_probs,
):
    r = lax.axis_index("resp")
    e = lax.axis_index("exp")
    z, x, c = r // 4, (r // 2) % 2, r % 2
    y, h = e // 2, e % 2

    cache = jnp.pad(prompt_cache, ((0, 0), (0, 0), (0, 640 - ENTRY)))
    keys = lax.all_gather(cache, "resp", axis=0, tiled=True)

    first_base = over_all(w_o.T, lambda z, x, c, y, h: (z, h, c, y, x))
    second_base = over_resp(first_base, 0, 1, 0)
    first_near = near_pieces(first_base, over_z)
    first_w = ring_pieces(first_base, first_near, over_z)
    second_near = near_pieces(second_base, over_z)
    second_w = ring_pieces(second_base, second_near, over_z)

    both = jnp.concatenate([expert_in[0, 0], expert_in[0, 1]], axis=1)

    first = gate_probs.astype(BF)
    second = (gate_probs - first.astype(F32)).astype(BF)
    third = (gate_probs - first.astype(F32) - second.astype(F32)).astype(BF)
    extra = jnp.concatenate([routes.astype(BF), first, second, third], axis=1)
    extra = jnp.pad(extra, ((0, 0), (0, 124)))
    extra = jnp.broadcast_to(extra[None], (8, BLOCK, 128))
    rest = residual.reshape(BLOCK, 8, SLICE).transpose(1, 0, 2)
    rest = jnp.concatenate([rest, extra], axis=2).reshape(8, 4 * BLOCK, 256)
    both = jnp.concatenate([both.reshape(8, SLICE, 256), rest], axis=1)
    both, _ = after(both, first_base)
    both = lax.all_to_all(
        both, "exp", split_axis=0, concat_axis=0, axis_index_groups=ALONG_Y, tiled=True
    ).reshape(NY, NH, WEIGHTS, 256)

    def half_of(which):
        return lax.dynamic_index_in_dim(both, which, 1, keepdims=False)


    values = attention(prompt_len, queries, keys, resp_latent, w_uv)
    values, _ = after(values, first_near + [second_base])
    others = over_exp(values, 0, 1)
    gone, _ = after(half_of(1 - h), [others] + second_near + first_w)
    come, kept = over_exp(gone, 0, 1), half_of(h)
    rest = [data[:, SLICE:] for data in (kept, come)]
    rest = jnp.stack(
        [jnp.where(h == 0, rest[0], rest[1]), jnp.where(h == 0, rest[1], rest[0])], axis=1
    ).reshape(GROUP, SLICE + 128)
    others, _ = after(others, second_near + first_w)
    heads = [values, over_resp(values, 0, 0, 1), others, over_resp(others, 0, 0, 1)]

    table = rest[:, SLICE].astype(jnp.int32).reshape(8, BLOCK)
    earlier = jnp.arange(BLOCK)[None, :] < jnp.arange(BLOCK)[:, None]
    same = (table[:, :, None] == table[:, None, :]) & earlier[None]
    rank = jnp.sum(same.astype(jnp.int32), axis=2)
    place = table * (8 * CAP) + jnp.arange(8, dtype=jnp.int32)[:, None] * CAP + rank
    place = place.reshape(1, GROUP)
    gain = lax.dynamic_slice_in_dim(norm_gain, e * SLICE, SLICE, 0).reshape(1, SLICE)
    own_same = (routes == routes[:, 0][None, :]) & earlier
    own_place = routes * (8 * CAP) + jnp.sum(own_same.astype(jnp.int32), axis=1, keepdims=True)

    match = jnp.where(h == x, 0, 1).reshape(1).astype(jnp.int32)
    pick = [((z - y - dy + 2 * NY) % NY).astype(jnp.int32) for dy in range(NY)]
    order = jnp.stack([pick[1], pick[3], pick[0]])
    match, order = after(match, order)
    top, bottom = project(match, jnp.stack(pick[2:3]), heads, first_w + second_w, True)
    from_left = over_exp(top, 1, 0)
    from_right = over_exp(bottom, 3, 0)
    pieces = project(match, order, heads, first_w + second_w)
    far0 = other_core(pieces[5], 0)
    merged, far0 = after(merge(pieces[:4], from_left, from_right), far0)
    near1, far1, near3, far3 = merged
    parts = [
        pieces[4],
        over_exp(near1, 1, 0),
        over_exp(near3, 3, 0),
        far0,
        other_core(far1, 1),
        other_core(far3, 3),
    ]
    core = c.reshape(1).astype(jnp.int32)
    sorted_rows = dispatch(core, parts, rest, place)
    tokens = lax.all_to_all(sorted_rows, "resp", split_axis=0, concat_axis=0, tiled=True)
    message = enter(h.reshape(1).astype(jnp.int32), tokens, gain, kept, come)
    message = lax.all_to_all(message, "exp", split_axis=0, concat_axis=0, tiled=True)
    act = activate(message)
    act = lax.all_to_all(act, "exp", split_axis=0, concat_axis=0, tiled=True)
    finished = leave(act, expert_out, tokens)
    finished = lax.all_to_all(
        finished.reshape(128, CAP, SLICE),
        ("resp", "exp"),
        split_axis=0,
        concat_axis=0,
        tiled=True,
    ).reshape(GROUP, SLICE)
    return restore(finished, own_place)


def solution(mesh):
    return jax.shard_map(
        body,
        mesh=mesh,
        in_specs=(
            P("resp", None, "exp"),
            P("resp", None, None),
            P("resp", None, None),
            P(),
            P("exp", None, None),
            P("exp", "resp"),
            P(("resp", "exp"), None),
            P(),
            P("resp", None, None, "exp"),
            P("resp", None, "exp"),
            P(("resp", "exp"), None),
            P(("resp", "exp"), None),
        ),
        out_specs=P(("resp", "exp"), None),
        check_vma=False,
    )
```

```python
import functools

import jax
import jax.numpy as jnp
from jax import lax
from jax.experimental import pallas as pl
from jax.experimental.pallas import tpu as pltpu
from jax.sharding import PartitionSpec as P

SCALE = 192.0 ** (-0.5)
ROUTED = 2.5
EPSILON = 1e-06
NEGATIVE = -1e30
NZ, NX, NC, NY, NH = 4, 2, 2, 4, 2
RLEN, ENTRY, LAT, PLEN, HEADS, VHEAD = 32, 576, 512, 128, 8, 128
DIM, SLICE, HALF, FF, HID = 7168, 896, 448, 1024, 128
GROUP, BLOCK, CAP = 512, 64, 4
BATCH = 4
TILES = 2 * FF // 128 + 1
WEIGHTS = SLICE + 4 * BLOCK
ALONG_Y = [[y * NH + h for y in range(NY)] for h in range(NH)]
BF = jnp.bfloat16
F32 = jnp.float32


def params(mebibytes):
    return pltpu.CompilerParams(vmem_limit_bytes=mebibytes * 1024 * 1024)


def resp_perm(dz, dx, dc):
    pairs = []
    for z in range(NZ):
        for x in range(NX):
            for c in range(NC):
                source = (z * NX + x) * NC + c
                target = (((z + dz) % NZ) * NX + (x ^ dx)) * NC + (c ^ dc)
                pairs.append((source, target))
    return pairs


def exp_perm(dy, dh):
    pairs = []
    for y in range(NY):
        for h in range(NH):
            pairs.append((y * NH + h, ((y + dy) % NY) * NH + (h ^ dh)))
    return pairs


def over_resp(x, dz, dx, dc):
    return lax.ppermute(x, "resp", resp_perm(dz, dx, dc))


def over_exp(x, dy, dh):
    return lax.ppermute(x, "exp", exp_perm(dy, dh))


def everywhere(move):
    def number(z, x, c, y, h):
        return ((z * NX + x) * NC + c) * (NY * NH) + y * NH + h

    return [
        (number(z, x, c, y, h), number(*move(z, x, c, y, h)))
        for z in range(NZ)
        for x in range(NX)
        for c in range(NC)
        for y in range(NY)
        for h in range(NH)
    ]


def over_all(x, move):
    return lax.ppermute(x, ("resp", "exp"), everywhere(move))


def other_core(x, step):
    return over_all(x, lambda z, x, c, y, h: (z, x, 1 - c, (y + step) % NY, h))


def over_z(x, step):
    return over_resp(x, step, 0, 0)


def over_y(x, step):
    return over_exp(x, step, 0)


def after(x, y):
    return lax.optimization_barrier((x, y))


def near_pieces(x, shift):
    return [shift(x, 1), shift(x, 3)]


def ring_pieces(x, near, shift):
    half = x.shape[0] // 2
    left, right = near
    return [x, left, shift(left[:half], 1), shift(right[half:], 3), right]


def dot(a, b):
    return lax.dot_general(a, b, (((1,), (0,)), ((), ())), preferred_element_type=F32)


def dot_nt(a, b):
    return lax.dot_general(a, b, (((1,), (1,)), ((), ())), preferred_element_type=F32)


def attention_kernel(lens, q_ref, keys, own, w_uv, out, lat, even, odd, bias):
    step = pl.program_id(0)
    rows = HEADS * RLEN
    total = PLEN + RLEN

    @pl.when(step == 0)
    def _():
        even[:, PLEN:, ENTRY:] = jnp.zeros((BATCH, RLEN, 640 - ENTRY), BF)
        odd[:, :, :64] = jnp.zeros((BATCH, total, 64), BF)
        column = lax.broadcasted_iota(jnp.int32, (rows, total), 1)
        token = lax.broadcasted_iota(jnp.int32, (rows, total), 0) % RLEN
        seen = (column < PLEN) | (column <= token + PLEN)
        bias[...] = jnp.where(seen, 0.0, NEGATIVE)

    for part in range(BATCH):
        resp = BATCH * step + part
        even[part, :PLEN, :] = keys[part]
        even[part, PLEN:, :ENTRY] = own[part]
        odd[part, :PLEN, 64:] = keys[part, :, :ENTRY]
        odd[part, PLEN:, 64:] = own[part]
        first = [q_ref[part, :, p * 1152 : p * 1152 + 640] for p in range(HEADS // 2)]
        second = [q_ref[part, :, p * 1152 + 512 : p * 1152 + 1152] for p in range(HEADS // 2)]
        scores = jnp.concatenate(
            [
                dot_nt(jnp.concatenate(first, axis=0), even[part]),
                dot_nt(jnp.concatenate(second, axis=0), odd[part]),
            ],
            axis=0,
        )
        column = lax.broadcasted_iota(jnp.int32, (1, total), 1)
        dead = (column >= lens[resp]) & (column < PLEN)
        scores = scores + (bias[...] + jnp.where(dead, NEGATIVE, 0.0))
        peak = jnp.max(scores, axis=1, keepdims=True)
        weights = jnp.exp((scores - peak) * SCALE)
        probs = (weights * (1.0 / jnp.sum(weights, axis=1, keepdims=True))).astype(BF)
        latent = dot(probs, even[part, :, :LAT]).astype(BF)
        start = pl.multiple_of(resp * RLEN, RLEN)
        for p in range(HEADS // 2):
            lat[2 * p, pl.ds(start, RLEN), :] = latent[p * RLEN : (p + 1) * RLEN]
            lat[2 * p + 1, pl.ds(start, RLEN), :] = latent[
                rows // 2 + p * RLEN : rows // 2 + (p + 1) * RLEN
            ]

    @pl.when(step == pl.num_programs(0) - 1)
    def _():
        for head in range(HEADS):
            out[:, head * VHEAD : (head + 1) * VHEAD] = dot(lat[head], w_uv[head]).astype(BF)


def attention(lens, queries, keys, own, w_uv):
    count = queries.shape[0]
    spec = pltpu.PrefetchScalarGridSpec(
        num_scalar_prefetch=1,
        grid=(count // BATCH,),
        in_specs=[
            pl.BlockSpec((BATCH, RLEN, HEADS * ENTRY), lambda i, n: (i, 0, 0)),
            pl.BlockSpec((BATCH, PLEN, 640), lambda i, n: (i, 0, 0)),
            pl.BlockSpec((BATCH, RLEN, ENTRY), lambda i, n: (i, 0, 0)),
            pl.BlockSpec((HEADS, LAT, VHEAD), lambda i, n: (0, 0, 0)),
        ],
        out_specs=pl.BlockSpec((GROUP, HEADS * VHEAD), lambda i, n: (0, 0)),
        scratch_shapes=[
            pltpu.VMEM((HEADS, GROUP, LAT), BF),
            pltpu.VMEM((BATCH, PLEN + RLEN, 640), BF),
            pltpu.VMEM((BATCH, PLEN + RLEN, 640), BF),
            pltpu.VMEM((HEADS * RLEN, PLEN + RLEN), F32),
        ],
    )
    return pl.pallas_call(
        attention_kernel,
        grid_spec=spec,
        out_shape=jax.ShapeDtypeStruct((GROUP, HEADS * VHEAD), BF),
        compiler_params=params(56),
        name="attention",
    )(lens, queries, keys, own, w_uv)


def project_kernel(count, by_rows, match, picks, *refs):
    heads, weights = refs[:4], refs[4:14]
    outs = refs[14 : 14 + 2 * count]
    v_all, w_all, v_sem, w_sem = refs[14 + 2 * count :]
    cut = HALF // 2

    def weight_copies(n, part, k):
        own = weights[5 * part : 5 * part + 5]
        copies = []
        for side in range(2):
            if k == 2:
                source = own[2 + side]
            else:
                source = own[min(k, 1) if k < 2 else 4].at[pl.ds(side * cut, cut)]
            target = w_all.at[n, part, pl.ds(side * cut, cut)]
            copies.append(pltpu.make_async_copy(source, target, w_sem.at[n, part, side]))
        return copies

    def start_weights(n):
        for k in range(NZ):

            @pl.when(picks[n] == k)
            def _():
                for part in range(2):
                    for copy in weight_copies(n, part, k):
                        copy.start()

    def head_copy(k):
        target = v_all.at[k // 2, pl.ds((k % 2) * GROUP, GROUP)]
        return pltpu.make_async_copy(heads[k], target, v_sem.at[k])

    start_weights(0)
    for k in range(4):
        head_copy(k).start()
    for n in range(1, count):
        start_weights(n)
    for k in range(4):
        head_copy(k).wait()
    for n in range(count):
        for part in range(2):
            for copy in weight_copies(n, part, 0):
                copy.wait()
        for core in range(2):
            total = None
            for part in range(2):
                group = v_all.at[match[0] if part == 0 else 1 - match[0]]
                term = dot_nt(w_all[n, part], group[core * GROUP : (core + 1) * GROUP, :])
                total = term if total is None else total + term
            total = total.astype(BF)
            if by_rows:
                for side in range(2):
                    outs[side][:, core * GROUP : (core + 1) * GROUP] = total[
                        side * cut : (side + 1) * cut
                    ]
            else:
                outs[2 * n + core][...] = total


def project(match, picks, heads, weights, by_rows=False):
    count = picks.shape[0]
    shape = (HALF // 2, 2 * GROUP) if by_rows else (HALF, GROUP)
    vmem = pl.BlockSpec(memory_space=pltpu.VMEM)
    smem = pl.BlockSpec(memory_space=pltpu.SMEM)
    anywhere = pl.BlockSpec(memory_space=pl.ANY)
    return pl.pallas_call(
        functools.partial(project_kernel, count, by_rows),
        in_specs=[smem, smem] + [anywhere] * 14,
        out_specs=[vmem] * (2 * count),
        out_shape=[jax.ShapeDtypeStruct(shape, BF)] * (2 * count),
        scratch_shapes=[
            pltpu.VMEM((2, 2 * GROUP, HEADS * VHEAD), BF),
            pltpu.VMEM((count, 2, HALF, HEADS * VHEAD), BF),
            pltpu.SemaphoreType.DMA((4,)),
            pltpu.SemaphoreType.DMA((count, 2, 2)),
        ],
        compiler_params=params(56),
        name="project",
    )(match, picks, *heads, *weights)


def merge_kernel(ahead0, ahead1, behind0, behind1, left, right, *outs):
    pieces = (ahead0, ahead1, behind0, behind1)
    for n, (piece, out) in enumerate(zip(pieces, outs)):
        arrived = left if n < 2 else right
        lanes = slice((n % 2) * GROUP, (n % 2 + 1) * GROUP)
        out[...] = (piece[...].astype(F32) + arrived[:, lanes].astype(F32)).astype(BF)


def merge(pieces, left, right):
    cut = HALF // 2
    upper = pl.BlockSpec((cut, GROUP), lambda i: (0, 0))
    lower = pl.BlockSpec((cut, GROUP), lambda i: (1, 0))
    whole = pl.BlockSpec((cut, 2 * GROUP), lambda i: (0, 0))
    return pl.pallas_call(
        merge_kernel,
        grid=(1,),
        in_specs=[upper, upper, lower, lower, whole, whole],
        out_specs=[upper, upper, lower, lower],
        out_shape=[jax.ShapeDtypeStruct((HALF, GROUP), BF)] * 4,
        input_output_aliases={0: 0, 1: 1, 2: 2, 3: 3},
        compiler_params=params(56),
        name="merge",
    )(*pieces, left, right)


def dispatch_kernel(core, near0, near1, near3, far0, far1, far3, rest, place, out, attended):
    near = near0[...].astype(F32) + near1[...].astype(F32) + near3[...].astype(F32)
    far = far0[...].astype(F32) + far1[...].astype(F32) + far3[...].astype(F32)
    lower = core[0] == 0
    attended[:HALF, :] = jnp.where(lower, near, far).astype(BF)
    attended[HALF:, :] = jnp.where(lower, far, near).astype(BF)
    rows = lax.broadcasted_iota(jnp.int32, (GROUP, GROUP), 0)
    select = jnp.where(rows == place[...], 1.0, 0.0).astype(BF)
    moved = dot(select, rest[...])
    out[:, :SLICE] = (moved[:, :SLICE] + dot_nt(select, attended[...])).astype(BF)
    out[:, SLICE:] = moved[:, SLICE:].astype(BF)


def dispatch(core, parts, rest, place):
    vmem = pl.BlockSpec(memory_space=pltpu.VMEM)
    return pl.pallas_call(
        dispatch_kernel,
        in_specs=[pl.BlockSpec(memory_space=pltpu.SMEM)] + [vmem] * 8,
        out_specs=vmem,
        out_shape=jax.ShapeDtypeStruct((GROUP, SLICE + 128), BF),
        scratch_shapes=[pltpu.VMEM((SLICE, GROUP), BF)],
        compiler_params=params(56),
        name="dispatch",
    )(core, *parts, rest, place)


def enter_kernel(half, tokens, gain, kept, come, out):
    hidden = tokens[:, :SLICE].astype(F32)
    square = jnp.sum(hidden * hidden, axis=1, keepdims=True)
    scaled = (hidden * gain[...]).astype(BF)

    def store(tile, value):
        for b in range(GROUP // BLOCK):
            start = pl.multiple_of((b * TILES + tile) * BLOCK, BLOCK)
            out[pl.ds(start, BLOCK), :] = value[b * BLOCK : (b + 1) * BLOCK]

    for k in range(NY):
        for weights, own in ((kept, half[0]), (come, 1 - half[0])):
            both = dot(scaled, weights[k, :SLICE, :]).astype(BF)
            for side in range(2):
                store((k * NH + own) * 2 + side, both[:, side * HID : (side + 1) * HID])
    high = square.astype(BF)
    low = (square - high.astype(F32)).astype(BF)
    lane = lax.broadcasted_iota(jnp.int32, (GROUP, 128), 1)
    store(TILES - 1, jnp.where(lane < 64, high.astype(F32), low.astype(F32)).astype(BF))


def enter(half, tokens, gain, kept, come):
    vmem = pl.BlockSpec(memory_space=pltpu.VMEM)
    return pl.pallas_call(
        enter_kernel,
        in_specs=[pl.BlockSpec(memory_space=pltpu.SMEM)] + [vmem] * 4,
        out_specs=vmem,
        out_shape=jax.ShapeDtypeStruct((GROUP * TILES, 128), BF),
        compiler_params=params(20),
        name="enter",
    )(half, tokens, gain, kept, come)


def act_kernel(parts, out):
    def total(tile):
        value = jnp.zeros((BLOCK, 128), F32)
        for k in range(GROUP // BLOCK):
            start = (k * TILES + tile) * BLOCK
            value = value + parts[start : start + BLOCK, :].astype(F32)
        return value

    square = total(TILES - 1)
    square = square[:, :1] + square[:, 64:65]
    scale = lax.rsqrt(square * (1.0 / DIM) + EPSILON)
    for k in range(FF // HID):
        gate = total(2 * k) * scale
        act = (gate / (1.0 + jnp.exp(-gate)) * (total(2 * k + 1) * scale)).astype(BF)
        for b in range(GROUP // BLOCK):
            out[b * BLOCK : (b + 1) * BLOCK, k * HID : (k + 1) * HID] = act


def activate(parts):
    vmem = pl.BlockSpec(memory_space=pltpu.VMEM)
    return pl.pallas_call(
        act_kernel,
        in_specs=[vmem],
        out_specs=vmem,
        out_shape=jax.ShapeDtypeStruct((GROUP, FF), BF),
        compiler_params=params(16),
        name="activate",
    )(parts)


def leave_kernel(act, w_out, tokens, out):
    result = dot(act[...], w_out[0]).astype(BF).astype(F32)
    parts = tokens[:, SLICE:].astype(F32)
    share = ROUTED * (parts[:, 1:2] + parts[:, 2:3] + parts[:, 3:4])
    out[...] = (tokens[:, :SLICE].astype(F32) + share * result).astype(BF)


def leave(act, w_out, tokens):
    vmem = pl.BlockSpec(memory_space=pltpu.VMEM)
    return pl.pallas_call(
        leave_kernel,
        in_specs=[vmem] * 3,
        out_specs=vmem,
        out_shape=jax.ShapeDtypeStruct((GROUP, SLICE), BF),
        compiler_params=params(16),
        name="leave",
    )(act, w_out, tokens)


def restore_kernel(rows, place, out, select):
    lane = lax.broadcasted_iota(jnp.int32, (BLOCK, GROUP), 1)
    count = DIM // SLICE
    for k in range(count):
        select[k * BLOCK : (k + 1) * BLOCK, :] = jnp.where(
            lane == place[...] + k * CAP, 1.0, 0.0
        ).astype(BF)
    moved = dot(select[...], rows[...]).astype(BF)
    for k in range(count):
        out[:, k * SLICE : (k + 1) * SLICE] = moved[k * BLOCK : (k + 1) * BLOCK]


def restore(rows, place):
    vmem = pl.BlockSpec(memory_space=pltpu.VMEM)
    return pl.pallas_call(
        restore_kernel,
        in_specs=[vmem] * 2,
        out_specs=vmem,
        out_shape=jax.ShapeDtypeStruct((BLOCK, DIM), BF),
        scratch_shapes=[pltpu.VMEM((GROUP, GROUP), BF)],
        compiler_params=params(8),
        name="restore",
    )(rows, place)


def body(
    queries,
    resp_latent,
    prompt_cache,
    prompt_len,
    w_uv,
    w_o,
    residual,
    norm_gain,
    expert_in,
    expert_out,
    routes,
    gate_probs,
):
    r = lax.axis_index("resp")
    e = lax.axis_index("exp")
    z, x, c = r // 4, (r // 2) % 2, r % 2
    y, h = e // 2, e % 2

    cache = jnp.pad(prompt_cache, ((0, 0), (0, 0), (0, 640 - ENTRY)))
    keys = lax.all_gather(cache, "resp", axis=0, tiled=True)

    first_base = over_all(w_o.T, lambda z, x, c, y, h: (z, h, c, y, x))
    second_base = over_resp(first_base, 0, 1, 0)
    first_near = near_pieces(first_base, over_z)
    first_w = ring_pieces(first_base, first_near, over_z)
    second_near = near_pieces(second_base, over_z)
    second_w = ring_pieces(second_base, second_near, over_z)

    both = jnp.concatenate([expert_in[0, 0], expert_in[0, 1]], axis=1)

    first = gate_probs.astype(BF)
    second = (gate_probs - first.astype(F32)).astype(BF)
    third = (gate_probs - first.astype(F32) - second.astype(F32)).astype(BF)
    extra = jnp.concatenate([routes.astype(BF), first, second, third], axis=1)
    extra = jnp.pad(extra, ((0, 0), (0, 124)))
    extra = jnp.broadcast_to(extra[None], (8, BLOCK, 128))
    rest = residual.reshape(BLOCK, 8, SLICE).transpose(1, 0, 2)
    rest = jnp.concatenate([rest, extra], axis=2).reshape(8, 4 * BLOCK, 256)
    both = jnp.concatenate([both.reshape(8, SLICE, 256), rest], axis=1)
    both, _ = after(both, first_base)
    both = lax.all_to_all(
        both, "exp", split_axis=0, concat_axis=0, axis_index_groups=ALONG_Y, tiled=True
    ).reshape(NY, NH, WEIGHTS, 256)

    def half_of(which):
        return lax.dynamic_index_in_dim(both, which, 1, keepdims=False)


    values = attention(prompt_len, queries, keys, resp_latent, w_uv)
    values, _ = after(values, first_near + [second_base])
    others = over_exp(values, 0, 1)
    gone, _ = after(half_of(1 - h), [others] + second_near + first_w)
    come, kept = over_exp(gone, 0, 1), half_of(h)
    rest = [data[:, SLICE:] for data in (kept, come)]
    rest = jnp.stack(
        [jnp.where(h == 0, rest[0], rest[1]), jnp.where(h == 0, rest[1], rest[0])], axis=1
    ).reshape(GROUP, SLICE + 128)
    others, _ = after(others, second_near + first_w)
    heads = [values, over_resp(values, 0, 0, 1), others, over_resp(others, 0, 0, 1)]

    table = rest[:, SLICE].astype(jnp.int32).reshape(8, BLOCK)
    earlier = jnp.arange(BLOCK)[None, :] < jnp.arange(BLOCK)[:, None]
    same = (table[:, :, None] == table[:, None, :]) & earlier[None]
    rank = jnp.sum(same.astype(jnp.int32), axis=2)
    place = table * (8 * CAP) + jnp.arange(8, dtype=jnp.int32)[:, None] * CAP + rank
    place = place.reshape(1, GROUP)
    gain = lax.dynamic_slice_in_dim(norm_gain, e * SLICE, SLICE, 0).reshape(1, SLICE)
    own_same = (routes == routes[:, 0][None, :]) & earlier
    own_place = routes * (8 * CAP) + jnp.sum(own_same.astype(jnp.int32), axis=1, keepdims=True)

    match = jnp.where(h == x, 0, 1).reshape(1).astype(jnp.int32)
    pick = [((z - y - dy + 2 * NY) % NY).astype(jnp.int32) for dy in range(NY)]
    order = jnp.stack([pick[1], pick[3], pick[0]])
    match, order = after(match, order)
    top, bottom = project(match, jnp.stack(pick[2:3]), heads, first_w + second_w, True)
    from_left = over_exp(top, 1, 0)
    from_right = over_exp(bottom, 3, 0)
    pieces = project(match, order, heads, first_w + second_w)
    far0 = other_core(pieces[5], 0)
    merged, far0 = after(merge(pieces[:4], from_left, from_right), far0)
    near1, far1, near3, far3 = merged
    parts = [
        pieces[4],
        over_exp(near1, 1, 0),
        over_exp(near3, 3, 0),
        far0,
        other_core(far1, 1),
        other_core(far3, 3),
    ]
    core = c.reshape(1).astype(jnp.int32)
    sorted_rows = dispatch(core, parts, rest, place)
    tokens = lax.all_to_all(sorted_rows, "resp", split_axis=0, concat_axis=0, tiled=True)
    message = enter(h.reshape(1).astype(jnp.int32), tokens, gain, kept, come)
    message = lax.all_to_all(message, "exp", split_axis=0, concat_axis=0, tiled=True)
    act = activate(message)
    act = lax.all_to_all(act, "exp", split_axis=0, concat_axis=0, tiled=True)
    finished = leave(act, expert_out, tokens)
    finished = lax.all_to_all(
        finished.reshape(128, CAP, SLICE),
        ("resp", "exp"),
        split_axis=0,
        concat_axis=0,
        tiled=True,
    ).reshape(GROUP, SLICE)
    return restore(finished, own_place)


def solution(mesh):
    return jax.shard_map(
        body,
        mesh=mesh,
        in_specs=(
            P("resp", None, "exp"),
            P("resp", None, None),
            P("resp", None, None),
            P(),
            P("exp", None, None),
            P("exp", "resp"),
            P(("resp", "exp"), None),
            P(),
            P("resp", None, None, "exp"),
            P("resp", None, "exp"),
            P(("resp", "exp"), None),
            P(("resp", "exp"), None),
        ),
        out_specs=P(("resp", "exp"), None),
        check_vma=False,
    )
```
